32 devices in a mesh: lon: 8 (over z, y), lat: 4 (over x, core).
Axes of the slice: x: 2, y: 2, z: 4, core: 2. Of those that a mesh axis runs over, the one named last changes fastest.
Arguments:
- spectra: float32 [25, 36, 32768], P(None, None, ('lon', 'lat')), may hold values from 0 to 1
- wind_growth: float32 [32768], P(('lon', 'lat')), may hold values from 0.05 to 0.6
- wind_dir: float32 [32768], P(('lon', 'lat')), may hold values from -3.140625 to 3.140625
- point_cell: int32 [32768], P(('lon', 'lat')), may hold values from -1 to 32767, as said below
- land_mask: int32 [16, 2048], P('lon', 'lat'), may hold values from 0 to 1, as said below
- shoaling: float32 [16, 2048], P('lon', 'lat'), may hold values from 0.5 to 1
- slope_x: float32 [16, 2048], P('lon', 'lat'), may hold values from -0.5 to 0.5
- slope_y: float32 [16, 2048], P('lon', 'lat'), may hold values from -0.5 to 0.5
Outputs:
- wave_field: float32 [25, 36, 16, 2048], P(None, None, 'lon', 'lat')
The draws below stay inside these ranges and needn't reach their ends.
Inputs may be any that keep to these rules, and one draw needn't show every extreme that they name: `point_cell`: every sea cell of land_mask is named by exactly one slot over all devices, land cells by none, other slots hold -1. The slots of one device name at most 32 cells of any one device's block of 2 x 512 cells, and in every draw some block gets exactly 32 from every device. `land_mask`: at least a quarter of the cells of each device's block are sea; some block is all sea.
All inputs are finite; a program needn't handle non-finite values.
Results may differ from the reference program's by a relative error of at most 0.0001.
Values sent between devices are 32-bit elements; how exact they have to be, the bound alone decides.
No kernel may reach another device: no remote copies, remote signals or barrier semaphores. Data moves between devices by JAX's collectives and lax.ppermute only.
A program may use at most 128 MiB of HBM per device.

```python
import math
import jax
import jax.numpy as jnp
from jax import lax

NF = 25
ND = 36
GX = 2
GY = 512
NSUB = 2
NX = 16
NY = 2048
POINTS = 32768
N_LON = 8
N_LAT = 4


def build_layout(key):
    devices = N_LON * N_LAT
    cells = GX * GY
    key_rank, key_count, key_full, key_shift, key_slot = jax.random.split(jax.random.fold_in(key, 11), 5)
    ranks = jax.vmap(lambda k: jax.random.permutation(k, cells))(jax.random.split(key_rank, devices))
    counts = jax.random.randint(key_count, (devices,), cells // 4, cells + 1)
    full = jax.random.randint(key_full, (), 0, devices)
    counts = jnp.where(jnp.arange(devices) == full, cells, counts)
    tile = jnp.arange(devices)[:, None]
    local = jnp.arange(cells)[None, :]
    corner = (tile == devices - 1) & (local == cells - 1)
    sea = (ranks < counts[:, None]) | corner
    lon_id = tile // N_LAT
    lat_id = tile % N_LAT
    glob_x = lon_id * GX + local // GY
    glob_y = lat_id * GY + local % GY
    cell_id = (glob_x * (GY * N_LAT) + glob_y).astype(jnp.int32)
    shift = jax.random.randint(key_shift, (devices, 1), 0, devices)
    source = (ranks + shift) % devices
    canon = tile * (cells // devices) + ranks // devices
    flat_target = jnp.where(sea, source * cells + canon, devices * cells)
    holder = jnp.full((devices * cells,), -1, jnp.int32)
    holder = holder.at[flat_target.reshape(-1)].set(cell_id.reshape(-1), mode='drop').reshape(devices, cells)
    perms = jax.vmap(lambda k: jax.random.permutation(k, cells))(jax.random.split(key_slot, devices))
    inverse = jnp.argsort(perms, axis=1)
    shuffled = jnp.take_along_axis(holder, inverse, axis=1)
    return (sea, shuffled)


def draw_point_cell(key, part):
    sea, shuffled = build_layout(key)
    return shuffled.reshape(-1).astype(jnp.int32)


def draw_land_mask(key, part):
    sea, shuffled = build_layout(key)
    grid = sea.astype(jnp.int32).reshape(N_LON, N_LAT, GX, GY)
    return jnp.transpose(grid, (0, 2, 1, 3)).reshape(GX * N_LON, GY * N_LAT)


def draw_spectra(key, part):
    key_scale, key_entry = jax.random.split(jax.random.fold_in(key, 23), 2)
    total = GX * GY * N_LON * N_LAT
    scale = jnp.exp(jax.random.uniform(key_scale, (total,), jnp.float32, math.log(0.1), 0.0))
    entries = jax.random.uniform(key_entry, (NF, ND, total), jnp.float32, 0.1, 1.0)
    return (entries * scale[None, None, :]).astype(jnp.float32)


def levels(own_key, extent, cuts, least, largest):
    factor_of = 1.0
    for position, parts in cuts:
        heights = jax.random.uniform(jax.random.fold_in(jax.random.fold_in(own_key, 6), position), (parts,), jnp.float32, least / len(cuts), largest / len(cuts))
        factor_of = factor_of * jnp.repeat(jnp.exp(heights), extent[position] // parts).reshape((-1,) + (1,) * (len(extent) - 1 - position))
    return factor_of


def setup_inputs(seed: int = 0) -> dict:
    key_list = jax.random.split(jax.random.key(seed), 9)
    return {
        "spectra": draw_spectra(jax.random.fold_in(key_list[8], 71), 0),
        "wind_growth": jnp.clip(jnp.exp(math.log(0.6) - 2.4849067 * jax.random.uniform(key_list[1], (POINTS,), jnp.float32) ** levels(key_list[1], (POINTS,), ((0, 32),), -0.2, 0.2)), 0.05, 0.6),
        "wind_dir": jnp.clip(jax.random.uniform(key_list[2], (POINTS,), jnp.float32, -3.140625, 3.140625), -3.140625, 3.140625),
        "point_cell": draw_point_cell(jax.random.fold_in(key_list[8], 71), 0),
        "land_mask": draw_land_mask(jax.random.fold_in(key_list[8], 71), 0),
        "shoaling": jnp.clip(0.5 + 0.5 * jax.random.uniform(key_list[5], (NX, NY), jnp.float32) ** levels(key_list[5], (NX, NY), ((0, 8), (1, 4)), -0.2, 0.2), 0.5, 1.0),
        "slope_x": jnp.clip(jax.random.uniform(key_list[6], (NX, NY), jnp.float32, -0.5, 0.5) * levels(key_list[6], (NX, NY), ((0, 8), (1, 4)), -0.4, 0.0), -0.5, 0.5),
        "slope_y": jnp.clip(jax.random.uniform(key_list[7], (NX, NY), jnp.float32, -0.5, 0.5) * levels(key_list[7], (NX, NY), ((0, 8), (1, 4)), -0.4, 0.0), -0.5, 0.5),
    }


def spectral_tables(nfreq, ndir):
    level = jnp.arange(nfreq, dtype=jnp.float32)
    ratio = 1.1 ** (level - (nfreq - 1))
    speed = 0.65 * 1.1 ** (-level)
    width = 0.1 * 1.1 ** level
    theta = (jnp.arange(ndir, dtype=jnp.float32) + 0.5) * (2.0 * math.pi / ndir)
    return ratio, speed, width, theta


def propagate(field, speed_f, shoaling, slope_x, slope_y, sea, cos_t, sin_t):
    cx = speed_f * shoaling[None] * cos_t[:, None, None]
    cy = speed_f * shoaling[None] * sin_t[:, None, None]
    turn = speed_f * (sin_t[:, None, None] * slope_x[None] - cos_t[:, None, None] * slope_y[None])
    for step in range(NSUB):
        qx = cx * field
        qy = cy * field
        flux_x = jnp.maximum(qx, 0.0) + jnp.minimum(jnp.roll(qx, -1, axis=1), 0.0)
        net_x = flux_x - jnp.roll(flux_x, 1, axis=1)
        padq = jnp.pad(qy, ((0, 0), (0, 0), (1, 1)))
        flux_y = jnp.maximum(padq[:, :, :-1], 0.0) + jnp.minimum(padq[:, :, 1:], 0.0)
        net_y = flux_y[:, :, 1:] - flux_y[:, :, :-1]
        half = field - net_x - net_y
        qt = turn * half
        flux_t = jnp.maximum(qt, 0.0) + jnp.minimum(jnp.roll(qt, -1, axis=0), 0.0)
        field = (half - flux_t + jnp.roll(flux_t, 1, axis=0)) * sea
    return field


def reference(spectra, wind_growth, wind_dir, point_cell, land_mask, shoaling, slope_x, slope_y):
    ratio, speed, width, theta = spectral_tables(NF, ND)
    dtheta = 2.0 * math.pi / ND

    def accumulate(f, total):
        return total + width[f] * dtheta * jnp.sum(spectra[f], axis=0)

    energy = lax.fori_loop(0, NF, accumulate, jnp.zeros((POINTS,), jnp.float32))
    load = energy / (energy + 10.0)
    lobe = jnp.maximum(jnp.cos(theta[:, None] - wind_dir[None, :]), 0.0) ** 2
    target = jnp.where(point_cell >= 0, point_cell, NX * NY).astype(jnp.int32)
    sea = land_mask.astype(jnp.float32)
    cos_t = jnp.cos(theta)
    sin_t = jnp.sin(theta)

    def one_frequency(inputs):
        spec_f, speed_f, ratio_f = inputs
        rate = wind_growth[None, :] * lobe * ratio_f - 0.4 * ratio_f * load[None, :]
        sourced = spec_f * jnp.exp(rate)
        grid = jnp.zeros((ND, NX * NY + 1), jnp.float32).at[:, target].set(sourced)
        grid = grid[:, :NX * NY].reshape(ND, NX, NY)
        return propagate(grid, speed_f, shoaling, slope_x, slope_y, sea, cos_t, sin_t)

    return lax.map(one_frequency, (spectra, speed, ratio))
```

```python
import functools
import math

import jax
import jax.numpy as jnp
import numpy as np
from jax import lax
from jax.experimental import pallas as pl
from jax.experimental.pallas import tpu as pltpu
from jax.sharding import PartitionSpec as P

F32 = jnp.float32
BF16 = jnp.bfloat16
NSUB = 2
LANES = 128
SUB = 8
CHUNKS = (9, 8, 8)
NBLOCK = 256
VMEM_LIMIT = 32 * 2**20


def ceil_to(value, step):
    return -(-value // step) * step


def divide(value, count):
    if count & (count - 1) == 0:
        return value >> (count.bit_length() - 1), value & (count - 1)
    quotient = value // count
    return quotient, value - quotient * count


class Plan:
    def __init__(self, count, ndir, cap, labels):
        self.cap = cap
        self.parts = LANES // cap
        self.rows = count * ndir + (1 if labels else 0)
        self.per = -(-self.rows // self.parts)
        self.padded = ceil_to(self.per, SUB)
        self.total = self.parts * self.padded
        self.label_row = (
            count * ndir // self.per * self.padded + count * ndir % self.per if labels else None
        )

    def pieces(self, start, length):
        found = []
        at = start
        while at < start + length:
            part, inside = divmod(at, self.per)
            take = min(self.per - inside, start + length - at)
            found.append((at - start, part * self.padded + inside, take))
            at += take
        return found


def swap_blocks(blocks, cap):
    parts = len(blocks)
    lane = lax.broadcasted_iota(jnp.int32, blocks[0].shape, 1)
    rolled = [pltpu.roll(b, cap * q, 1) if q else b for q, b in enumerate(blocks)]
    result = []
    for i in range(parts):
        mixed = rolled[-i % parts]
        for j in range(1, parts):
            mixed = jnp.where(lane >= j * cap, rolled[(j - i) % parts], mixed)
        result.append(pltpu.roll(mixed, LANES - cap * i, 1) if i else mixed)
    return result


def split_rows(x_ref, pair_ref):
    total = x_ref.shape[0]
    whole = x_ref[...]
    high = whole.astype(BF16)
    pair_ref[0:total, :] = high
    pair_ref[total : 2 * total, :] = (whole - high.astype(F32)).astype(BF16)


def route(pair_ref, picks, first):
    slots = pair_ref.shape[1]
    total = pair_ref.shape[0] // 2
    wanted = lax.broadcasted_iota(jnp.int32, (NBLOCK, slots), 0) + first
    onehot = jnp.where(wanted == picks, 1.0, 0.0).astype(BF16)
    both = lax.dot_general(
        pair_ref[...], onehot, (((1,), (1,)), ((), ())), preferred_element_type=F32
    )
    return both[:total] + both[total:]


def send_rows(plan, pair_ref, target, out_ref):
    slots = pair_ref.shape[1]
    groups = NBLOCK // LANES
    for block in range(slots // NBLOCK):
        moved = route(pair_ref, target, block * NBLOCK)
        for g in range(groups):
            blocks = [
                moved[q * plan.padded : (q + 1) * plan.padded, g * LANES : (g + 1) * LANES]
                for q in range(plan.parts)
            ]
            for i, message in enumerate(swap_blocks(blocks, plan.cap)):
                out_ref[(block * groups + g) * plan.parts + i] = message


def source_rows(plan, spectra_ref, first, count, nfreq, gain, x_ref):
    ndir = spectra_ref.shape[1]
    for f in range(count):
        ratio = float(np.float32(1.1) ** np.float32(first + f - (nfreq - 1)))
        rows = spectra_ref[f] * jnp.exp(gain * ratio)
        for offset, row, length in plan.pieces(f * ndir, ndir):
            x_ref[row : row + length, :] = rows[offset : offset + length]


def first_source_kernel(
    plan, count, shape, spectra_ref, growth_ref, dir_ref, cell_ref,
    out_ref, gain_ref, target_ref, x_ref, pair_ref,
):
    rows_x, rows_y, lat_count, devices = shape
    nfreq, ndir, slots = spectra_ref.shape
    dtheta = 2.0 * math.pi / ndir
    total = None
    for f in range(nfreq):
        width = float(np.float32(0.1) * np.float32(1.1) ** np.float32(f)) * dtheta
        term = spectra_ref[f] * width
        total = term if total is None else total + term
    energy = jnp.sum(total, axis=0, keepdims=True)
    load = energy / (energy + 10.0)
    theta = (lax.broadcasted_iota(jnp.int32, (ndir, slots), 0).astype(F32) + 0.5) * dtheta
    lobe = jnp.maximum(jnp.cos(theta - dir_ref[...]), 0.0)
    gain = growth_ref[...] * (lobe * lobe) - 0.4 * load
    gain_ref[...] = gain

    point = cell_ref[...]
    valid = point >= 0
    col_x, col_y = divide(jnp.maximum(point, 0), rows_y * lat_count)
    own_x, in_x = divide(col_x, rows_x)
    own_y, in_y = divide(col_y, rows_y)
    owner = jnp.where(valid, own_x * lat_count + own_y, devices)
    band, lane = divide(in_y, LANES)
    label = jnp.where(valid, (band * rows_x + in_x) * LANES + lane + 1, 0).astype(F32)
    ids = lax.broadcasted_iota(jnp.int32, (devices, slots), 0)
    hits = jnp.where(ids == owner, 1.0, 0.0)
    lower = lax.broadcasted_iota(jnp.int32, (LANES, LANES), 0) < lax.broadcasted_iota(
        jnp.int32, (LANES, LANES), 1
    )
    ahead = jnp.where(lower, 1.0, 0.0).astype(BF16)
    carry = jnp.zeros((devices, 1), F32)
    places = []
    for b in range(slots // LANES):
        part = hits[:, b * LANES : (b + 1) * LANES]
        before = jnp.dot(part.astype(BF16), ahead, preferred_element_type=F32) + carry
        places.append(jnp.sum(before * part, axis=0, keepdims=True))
        carry = carry + jnp.sum(part, axis=1, keepdims=True)
    place = jnp.concatenate(places, axis=1).astype(jnp.int32)
    target = jnp.where(valid, owner * plan.cap + place, slots)
    target_ref[...] = target

    source_rows(plan, spectra_ref, 0, count, nfreq, gain, x_ref)
    x_ref[plan.label_row : plan.label_row + 1, :] = label
    split_rows(x_ref, pair_ref)
    send_rows(plan, pair_ref, target, out_ref)


def later_source_kernel(
    plan, first, count, nfreq, spectra_ref, gain_ref, target_ref, out_ref, x_ref, pair_ref
):
    source_rows(plan, spectra_ref, first, count, nfreq, gain_ref[...], x_ref)
    split_rows(x_ref, pair_ref)
    send_rows(plan, pair_ref, target_ref[...], out_ref)


def as_tile(grid_ref):
    grid = grid_ref[...].astype(F32)
    bands = grid.shape[1] // LANES
    return jnp.concatenate([grid[:, b * LANES : (b + 1) * LANES] for b in range(bands)], axis=0)


def tile_ids():
    return (
        lax.broadcasted_iota(jnp.int32, (SUB, LANES), 0),
        lax.broadcasted_iota(jnp.int32, (SUB, LANES), 1),
    )


def edge_messages(read, weight, f, ndir, right_ref, left_ref, up_ref, down_ref):
    row, lane = tile_ids()
    odd = (row & 1) == 1
    quarter = ndir // 4
    up = jnp.zeros((SUB, LANES), F32)
    down = jnp.zeros((SUB, LANES), F32)
    moved = [read(d) * weight for d in range(ndir)]
    for e in range(quarter):
        a, b = moved[3 * quarter + e], moved[e]
        right_ref[f, e] = jnp.where(odd, b, pltpu.roll(a, SUB - 1, 0))
        a, b = moved[quarter + e], moved[2 * quarter + e]
        left_ref[f, e] = jnp.where(odd, pltpu.roll(b, 1, 0), a)
    for k in range(2 * quarter):
        up = jnp.where(lane == k, pltpu.roll(moved[k], k + 1, 1), up)
        low = moved[2 * quarter + k]
        down = jnp.where(lane == k, pltpu.roll(low, k, 1) if k else low, down)
    up_ref[f] = up
    down_ref[f] = down


def place_kernel(plan, first, count, ndir, with_labels, *refs):
    if with_labels:
        in_ref, speed_ref, shoal_ref, *refs = refs
        own_ref, right_ref, left_ref, up_ref, down_ref, label_ref, x_ref, pair_ref = refs
    else:
        in_ref, speed_ref, shoal_ref, label_ref, *refs = refs
        own_ref, right_ref, left_ref, up_ref, down_ref, x_ref, pair_ref = refs
    slots = x_ref.shape[1]
    for g in range(slots // LANES):
        blocks = [in_ref[g * plan.parts + i] for i in range(plan.parts)]
        for q, part in enumerate(swap_blocks(blocks, plan.cap)):
            x_ref[q * plan.padded : (q + 1) * plan.padded, g * LANES : (g + 1) * LANES] = part
    if with_labels:
        label_ref[...] = x_ref[plan.label_row : plan.label_row + 1, :].astype(jnp.int32) - 1
    label = label_ref[...]
    split_rows(x_ref, pair_ref)
    for block in range(slots // NBLOCK):
        placed = route(pair_ref, label, block * NBLOCK)
        for t in range(NBLOCK // LANES):
            row = block * (NBLOCK // LANES) + t
            for q in range(plan.parts):
                length = min(plan.per, count * ndir - q * plan.per)
                if length > 0:
                    own_ref[pl.ds(q * plan.per * SUB + row, length, stride=SUB), :] = placed[
                        q * plan.padded : q * plan.padded + length, t * LANES : (t + 1) * LANES
                    ]
    shoal = as_tile(shoal_ref)

    @pl.loop(0, count)
    def pack(f):
        def read(d):
            return own_ref[pl.ds(pl.multiple_of((f * ndir + d) * SUB, SUB), SUB), :]

        edge_messages(
            read, shoal * speed_ref[first + f], f, ndir, right_ref, left_ref, up_ref, down_ref
        )


def step_kernel(first, last, *refs):
    (own_ref, right_in, left_in, up_in, down_in, speed_ref,
     shoal_ref, slope_x_ref, slope_y_ref, mask_ref, *refs) = refs
    if last:
        *refs, new_ref, turn_ref, done_sem = refs
        out_ref = refs[-1]
    else:
        new_ref, right_ref, left_ref, up_ref, down_ref, turn_ref = refs
    count, ndir = own_ref.shape[:2]
    quarter = ndir // 4
    row, lane = tile_ids()
    odd = (row & 1) == 1
    shoal = as_tile(shoal_ref)
    slope_x = as_tile(slope_x_ref)
    slope_y = as_tile(slope_y_ref)
    sea = as_tile(mask_ref)
    angle = [(d + 0.5) * (2.0 * math.pi / ndir) for d in range(ndir)]
    cos = [math.cos(a) for a in angle]
    sin = [math.sin(a) for a in angle]
    for d in range(ndir):
        turn_ref[d] = sin[d] * slope_x - cos[d] * slope_y

    @pl.loop(0, count)
    def advance(f):
        speed = speed_ref[first + f]
        weight = shoal * speed
        up_all = up_in[f]
        down_all = down_in[f]

        def halved(d):
            field = own_ref[f, d]
            moved = weight * field
            if d >= 3 * quarter or d < quarter:
                edge = right_in[f, d % quarter]
                if d < quarter:
                    edge = pltpu.roll(edge, SUB - 1, 0)
                from_x = jnp.where(odd, pltpu.roll(moved, 1, 0), edge)
            else:
                edge = left_in[f, d % quarter]
                if d < 2 * quarter:
                    edge = pltpu.roll(edge, 1, 0)
                from_x = jnp.where(odd, edge, pltpu.roll(moved, SUB - 1, 0))
            if d < 2 * quarter:
                near = pltpu.roll(moved, 1, 1)
                edge = pltpu.roll(up_all, LANES - d, 1) if d else up_all
                far = pltpu.roll(jnp.where(row >= SUB - 2, edge, near), 2, 0)
                from_y = jnp.where(lane == 0, far, near)
            else:
                near = pltpu.roll(moved, LANES - 1, 1)
                edge = pltpu.roll(down_all, LANES - 1 - (d - 2 * quarter), 1)
                far = pltpu.roll(jnp.where(row < 2, edge, near), SUB - 2, 0)
                from_y = jnp.where(lane == LANES - 1, far, near)
            along, across = abs(cos[d]), abs(sin[d])
            half = field - (along + across) * moved + along * from_x + across * from_y
            return half, turn_ref[d] * (half * speed)

        half_top, qt_top = halved(ndir - 1)
        half, qt = halved(0)
        below = jnp.maximum(qt_top, 0.0) + jnp.minimum(qt, 0.0)
        flux_top = below
        for d in range(ndir):
            if d < ndir - 2:
                half_next, qt_next = halved(d + 1)
            else:
                half_next, qt_next = half_top, qt_top
            if d < ndir - 1:
                above = jnp.maximum(qt, 0.0) + jnp.minimum(qt_next, 0.0)
            else:
                above = flux_top
            new_ref[f, d] = (half - above + below) * sea
            half, qt, below = half_next, qt_next, above
        if not last:
            edge_messages(
                lambda d: new_ref[f, d], weight, f, ndir, right_ref, left_ref, up_ref, down_ref
            )

    if last:
        copy = pltpu.make_async_copy(new_ref, out_ref.at[pl.ds(first, count)], done_sem)
        copy.start()
        copy.wait()


def params():
    return pltpu.CompilerParams(vmem_limit_bytes=VMEM_LIMIT)


def vmem(count):
    return [pl.BlockSpec(memory_space=pltpu.VMEM)] * count


SMEM_SPEC = pl.BlockSpec(memory_space=pltpu.SMEM)
ANY_SPEC = pl.BlockSpec(memory_space=pl.ANY)


def edge_shapes(count, ndir):
    tile = jax.ShapeDtypeStruct((count, ndir // 4, SUB, LANES), F32)
    line = jax.ShapeDtypeStruct((count, SUB, LANES), F32)
    return [tile, tile, line, line]


def send_edges(edges):
    right, left, up, down = edges
    lon = lax.axis_size("lon")
    lat = lax.axis_size("lat")
    return (
        lax.ppermute(right, "lon", [(i, (i + 1) % lon) for i in range(lon)]),
        lax.ppermute(left, "lon", [((i + 1) % lon, i) for i in range(lon)]),
        lax.ppermute(up, "lat", [(i, i + 1) for i in range(lat - 1)]),
        lax.ppermute(down, "lat", [(i + 1, i) for i in range(lat - 1)]),
    )


def on_device(spectra, wind_growth, wind_dir, point_cell, land_mask, shoaling, slope_x, slope_y):
    nfreq, ndir, slots = spectra.shape
    rows_x, rows_y = land_mask.shape
    lat_count = lax.axis_size("lat")
    devices = lax.axis_size("lon") * lat_count
    cap = slots // devices
    speed = jnp.asarray((0.65 * 1.1 ** -np.arange(nfreq)).astype(np.float32))
    starts = [sum(CHUNKS[:i]) for i in range(len(CHUNKS))]
    plans = [Plan(count, ndir, cap, i == 0) for i, count in enumerate(CHUNKS)]

    messages = []
    for i, (first, count, plan) in enumerate(zip(starts, CHUNKS, plans)):
        shape = jax.ShapeDtypeStruct((devices, plan.padded, LANES), F32)
        scratch = [
            pltpu.VMEM((plan.total, slots), F32),
            pltpu.VMEM((2 * plan.total, slots), BF16),
        ]
        if i == 0:
            message, gain, target = pl.pallas_call(
                functools.partial(
                    first_source_kernel, plan, count, (rows_x, rows_y, lat_count, devices)
                ),
                out_shape=[
                    shape,
                    jax.ShapeDtypeStruct((ndir, slots), F32),
                    jax.ShapeDtypeStruct((1, slots), jnp.int32),
                ],
                in_specs=vmem(4),
                out_specs=vmem(3),
                scratch_shapes=scratch,
                compiler_params=params(),
                name="source_first",
            )(
                spectra,
                wind_growth.reshape(1, slots),
                wind_dir.reshape(1, slots),
                point_cell.reshape(1, slots),
            )
        else:
            message = pl.pallas_call(
                functools.partial(later_source_kernel, plan, first, count, nfreq),
                out_shape=shape,
                in_specs=[pl.BlockSpec((pl.Element(count), pl.Element(ndir), pl.Element(slots)), lambda i, s=first: (s, 0, 0))]
                + [pl.BlockSpec((ndir, slots), lambda i: (0, 0)), pl.BlockSpec((1, slots), lambda i: (0, 0))],
                out_specs=pl.BlockSpec(shape.shape, lambda i: (0, 0, 0)),
                grid=(1,),
                scratch_shapes=scratch,
                compiler_params=params(),
                name="source_later",
            )(spectra, gain, target)
        messages.append(message)

    out = None
    label = None
    for i, (first, count, plan) in enumerate(zip(starts, CHUNKS, plans)):
        arrived = lax.all_to_all(
            messages[i], ("lon", "lat"), split_axis=0, concat_axis=0, tiled=True
        )
        edges = edge_shapes(count, ndir)
        own_shape = jax.ShapeDtypeStruct((count * ndir * SUB, LANES), F32)
        label_shape = jax.ShapeDtypeStruct((1, slots), jnp.int32)
        placed = pl.pallas_call(
            functools.partial(place_kernel, plan, first, count, ndir, i == 0),
            out_shape=[own_shape] + edges + ([label_shape] if i == 0 else []),
            in_specs=vmem(1) + [SMEM_SPEC] + vmem(1 if i == 0 else 2),
            out_specs=vmem(6 if i == 0 else 5),
            scratch_shapes=[
                pltpu.VMEM((plan.total, slots), F32),
                pltpu.VMEM((2 * plan.total, slots), BF16),
            ],
            compiler_params=params(),
            name="place",
        )(arrived, speed, shoaling, *([] if i == 0 else [label]))
        if i == 0:
            *placed, label = placed
        field, *sent = placed
        field = field.reshape(count, ndir, SUB, LANES)
        for step in range(NSUB):
            last = step == NSUB - 1
            received = send_edges(sent)
            whole = jax.ShapeDtypeStruct((nfreq, ndir, SUB, LANES), F32)
            same = jax.ShapeDtypeStruct(field.shape, F32)
            tables = [pltpu.VMEM((ndir, SUB, LANES), F32)]
            chained = last and out is not None
            result = pl.pallas_call(
                functools.partial(step_kernel, first, last),
                out_shape=whole if last else [same] + edges,
                in_specs=vmem(5) + [SMEM_SPEC] + vmem(4) + ([ANY_SPEC] if chained else []),
                out_specs=ANY_SPEC if last else vmem(5),
                scratch_shapes=(
                    [pltpu.VMEM(field.shape, F32)] + tables + [pltpu.SemaphoreType.DMA(())]
                    if last
                    else tables
                ),
                input_output_aliases={10: 0} if chained else {},
                compiler_params=params(),
                name="last_step" if last else "step",
            )(
                field, *received, speed, shoaling, slope_x, slope_y, land_mask,
                *([out] if chained else []),
            )
            if last:
                out = result
            else:
                field, *sent = result
    bands = rows_y // LANES
    out = out.reshape(nfreq, ndir, bands, rows_x, LANES)
    return out.transpose(0, 1, 3, 2, 4).reshape(nfreq, ndir, rows_x, rows_y)


def solution(mesh):
    placed = (
        P(None, None, ("lon", "lat")),
        P(("lon", "lat")),
        P(("lon", "lat")),
        P(("lon", "lat")),
        P("lon", "lat"),
        P("lon", "lat"),
        P("lon", "lat"),
        P("lon", "lat"),
    )
    return jax.shard_map(
        on_device,
        mesh=mesh,
        in_specs=placed,
        out_specs=P(None, None, "lon", "lat"),
        check_vma=False,
    )
```

```python
import functools
import math

import jax
import jax.numpy as jnp
import numpy as np
from jax import lax
from jax.experimental import pallas as pl
from jax.experimental.pallas import tpu as pltpu
from jax.sharding import PartitionSpec as P

F32 = jnp.float32
BF16 = jnp.bfloat16
LANES = 128
SUB = 8
CHUNKS = (9, 8, 8)
NBLOCK = 256
VMEM_LIMIT = 32 * 2**20


def ceil_to(value, step):
    return -(-value // step) * step


def divide(value, count):
    if count & (count - 1) == 0:
        return value >> (count.bit_length() - 1), value & (count - 1)
    quotient = value // count
    return quotient, value - quotient * count


class Plan:
    def __init__(self, count, ndir, cap, labels):
        self.cap = cap
        self.parts = LANES // cap
        self.rows = count * ndir + (1 if labels else 0)
        self.per = -(-self.rows // self.parts)
        self.padded = ceil_to(self.per, SUB)
        self.total = self.parts * self.padded
        self.label_row = (
            count * ndir // self.per * self.padded + count * ndir % self.per if labels else None
        )

    def pieces(self, start, length):
        found = []
        at = start
        while at < start + length:
            part, inside = divmod(at, self.per)
            take = min(self.per - inside, start + length - at)
            found.append((at - start, part * self.padded + inside, take))
            at += take
        return found


def swap_blocks(blocks, cap):
    parts = len(blocks)
    lane = lax.broadcasted_iota(jnp.int32, blocks[0].shape, 1)
    rolled = [pltpu.roll(b, cap * q, 1) if q else b for q, b in enumerate(blocks)]
    result = []
    for i in range(parts):
        mixed = rolled[-i % parts]
        for j in range(1, parts):
            mixed = jnp.where(lane >= j * cap, rolled[(j - i) % parts], mixed)
        result.append(pltpu.roll(mixed, LANES - cap * i, 1) if i else mixed)
    return result


def split_rows(x_ref, pair_ref):
    total = x_ref.shape[0]
    whole = x_ref[...]
    high = whole.astype(BF16)
    pair_ref[0:total, :] = high
    pair_ref[total : 2 * total, :] = (whole - high.astype(F32)).astype(BF16)


def route(pair_ref, picks, first):
    slots = pair_ref.shape[1]
    total = pair_ref.shape[0] // 2
    wanted = lax.broadcasted_iota(jnp.int32, (NBLOCK, slots), 0) + first
    onehot = jnp.where(wanted == picks, 1.0, 0.0).astype(BF16)
    both = lax.dot_general(
        pair_ref[...], onehot, (((1,), (1,)), ((), ())), preferred_element_type=F32
    )
    return both[:total] + both[total:]


def send_rows(plan, pair_ref, target, out_ref, done=None):
    slots = pair_ref.shape[1]
    groups = NBLOCK // LANES
    for block in range(slots // NBLOCK):
        moved = route(pair_ref, target, block * NBLOCK)
        for g in range(groups):
            blocks = [
                moved[q * plan.padded : (q + 1) * plan.padded, g * LANES : (g + 1) * LANES]
                for q in range(plan.parts)
            ]
            for i, message in enumerate(swap_blocks(blocks, plan.cap)):
                out_ref[(block * groups + g) * plan.parts + i] = message
        if done is not None:
            done(block)


def source_rows(plan, spectra_ref, first, count, nfreq, gain, x_ref):
    ndir = spectra_ref.shape[1]
    for f in range(count):
        ratio = float(np.float32(1.1) ** np.float32(first + f - (nfreq - 1)))
        rows = spectra_ref[f] * jnp.exp(gain * ratio)
        for offset, row, length in plan.pieces(f * ndir, ndir):
            x_ref[row : row + length, :] = rows[offset : offset + length]


PIECES = 5


def first_source_kernel(
    plan, count, shape, spectra_hbm, growth_hbm, dir_hbm, cell_hbm,
    out_hbm, gain_ref, target_ref,
    spectra_ref, growth_ref, dir_ref, cell_ref, x_ref, pair_ref, message_ref, sems, out_sems,
):
    rows_x, rows_y, lat_count, devices = shape
    nfreq, ndir, slots = spectra_ref.shape
    bounds = [nfreq * k // PIECES for k in range(PIECES + 1)]
    small = [
        pltpu.make_async_copy(src, dst, sems.at[PIECES + k])
        for k, (src, dst) in enumerate(
            ((cell_hbm, cell_ref), (growth_hbm, growth_ref), (dir_hbm, dir_ref))
        )
    ]
    pieces = [
        pltpu.make_async_copy(
            spectra_hbm.at[pl.ds(lo, hi - lo)], spectra_ref.at[pl.ds(lo, hi - lo)], sems.at[k]
        )
        for k, (lo, hi) in enumerate(zip(bounds, bounds[1:]))
    ]
    for copy in small + pieces:
        copy.start()
    small[0].wait()
    point = cell_ref[...]
    valid = point >= 0
    col_x, col_y = divide(jnp.maximum(point, 0), rows_y * lat_count)
    own_x, in_x = divide(col_x, rows_x)
    own_y, in_y = divide(col_y, rows_y)
    owner = jnp.where(valid, own_x * lat_count + own_y, devices)
    band, lane = divide(in_y, LANES)
    label = jnp.where(valid, (band * rows_x + in_x) * LANES + lane + 1, 0).astype(F32)
    ids = lax.broadcasted_iota(jnp.int32, (devices, slots), 0)
    hits = jnp.where(ids == owner, 1.0, 0.0)
    lower = lax.broadcasted_iota(jnp.int32, (LANES, LANES), 0) < lax.broadcasted_iota(
        jnp.int32, (LANES, LANES), 1
    )
    ahead = jnp.where(lower, 1.0, 0.0).astype(BF16)
    carry = jnp.zeros((devices, 1), F32)
    places = []
    for b in range(slots // LANES):
        part = hits[:, b * LANES : (b + 1) * LANES]
        before = jnp.dot(part.astype(BF16), ahead, preferred_element_type=F32) + carry
        places.append(jnp.sum(before * part, axis=0, keepdims=True))
        carry = carry + jnp.sum(part, axis=1, keepdims=True)
    place = jnp.concatenate(places, axis=1).astype(jnp.int32)
    target = jnp.where(valid, owner * plan.cap + place, slots)
    target_ref[...] = target

    small[1].wait()
    small[2].wait()
    dtheta = 2.0 * math.pi / ndir
    total = None
    for k, copy in enumerate(pieces):
        copy.wait()
        for f in range(bounds[k], bounds[k + 1]):
            width = float(np.float32(0.1) * np.float32(1.1) ** np.float32(f)) * dtheta
            term = spectra_ref[f] * width
            total = term if total is None else total + term
    energy = jnp.sum(total, axis=0, keepdims=True)
    load = energy / (energy + 10.0)
    theta = (lax.broadcasted_iota(jnp.int32, (ndir, slots), 0).astype(F32) + 0.5) * dtheta
    lobe = jnp.maximum(jnp.cos(theta - dir_ref[...]), 0.0)
    gain = growth_ref[...] * (lobe * lobe) - 0.4 * load
    gain_ref[...] = gain

    source_rows(plan, spectra_ref, 0, count, nfreq, gain, x_ref)
    x_ref[plan.label_row : plan.label_row + 1, :] = label
    split_rows(x_ref, pair_ref)
    copies = []

    def sent(block):
        per = devices * NBLOCK // slots
        part = pl.ds(block * per, per)
        copies.append(
            pltpu.make_async_copy(message_ref.at[part], out_hbm.at[part], out_sems.at[block])
        )
        copies[-1].start()

    send_rows(plan, pair_ref, target, message_ref, sent)
    for copy in copies:
        copy.wait()


def later_source_kernel(
    plan, first, count, nfreq, spectra_ref, gain_ref, target_ref, out_ref, x_ref, pair_ref
):
    source_rows(plan, spectra_ref, first, count, nfreq, gain_ref[...], x_ref)
    split_rows(x_ref, pair_ref)
    send_rows(plan, pair_ref, target_ref[...], out_ref)


def as_tile(grid_ref):
    grid = grid_ref[...].astype(F32)
    bands = grid.shape[1] // LANES
    return jnp.concatenate([grid[:, b * LANES : (b + 1) * LANES] for b in range(bands)], axis=0)


def tile_ids():
    return (
        lax.broadcasted_iota(jnp.int32, (SUB, LANES), 0),
        lax.broadcasted_iota(jnp.int32, (SUB, LANES), 1),
    )


def edge_messages(read, weight, odd_lon, f, ndir, pair_ref, cross_ref, side_ref):
    row, lane = tile_ids()
    odd = (row & 1) == 1
    quarter = ndir // 4
    up = jnp.zeros((SUB, LANES), F32)
    down = jnp.zeros((SUB, LANES), F32)
    moved = [read(d) * weight for d in range(ndir)]
    for e in range(quarter):
        a, b = moved[3 * quarter + e], moved[e]
        right = jnp.where(odd, b, pltpu.roll(a, SUB - 1, 0))
        a, b = moved[quarter + e], moved[2 * quarter + e]
        left = jnp.where(odd, pltpu.roll(b, 1, 0), a)
        pair_ref[f, e] = jnp.where(odd_lon, left, right)
        cross_ref[f, e] = jnp.where(odd_lon, right, left)
    for k in range(2 * quarter):
        up = jnp.where(lane == k, pltpu.roll(moved[k], k + 1, 1), up)
        low = moved[2 * quarter + k]
        down = jnp.where(lane == k, pltpu.roll(low, k, 1) if k else low, down)
    side_ref[f] = jnp.where(row >= SUB // 2, up, down)


def place_kernel(plan, first, count, ndir, with_labels, *refs):
    if with_labels:
        in_ref, speed_ref, ids_ref, shoal_ref, *refs = refs
        own_ref, right_ref, left_ref, side_ref, label_ref, x_ref, pair_ref = refs
    else:
        in_ref, speed_ref, ids_ref, shoal_ref, label_ref, *refs = refs
        refs = refs[-6:]
        own_ref, right_ref, left_ref, side_ref, x_ref, pair_ref = refs
    slots = x_ref.shape[1]
    for g in range(slots // LANES):
        blocks = [in_ref[g * plan.parts + i] for i in range(plan.parts)]
        for q, part in enumerate(swap_blocks(blocks, plan.cap)):
            x_ref[q * plan.padded : (q + 1) * plan.padded, g * LANES : (g + 1) * LANES] = part
    if with_labels:
        label_ref[...] = x_ref[plan.label_row : plan.label_row + 1, :].astype(jnp.int32) - 1
    label = label_ref[...]
    split_rows(x_ref, pair_ref)
    for block in range(slots // NBLOCK):
        placed = route(pair_ref, label, block * NBLOCK)
        for t in range(NBLOCK // LANES):
            row = block * (NBLOCK // LANES) + t
            for q in range(plan.parts):
                length = min(plan.per, count * ndir - q * plan.per)
                if length > 0:
                    own_ref[pl.ds(q * plan.per * SUB + row, length, stride=SUB), :] = placed[
                        q * plan.padded : q * plan.padded + length, t * LANES : (t + 1) * LANES
                    ]
    shoal = as_tile(shoal_ref)

    @pl.loop(0, count)
    def pack(f):
        def read(d):
            return own_ref[pl.ds(pl.multiple_of((f * ndir + d) * SUB, SUB), SUB), :]

        edge_messages(
            read, shoal * speed_ref[first + f], ids_ref[4] == 1, f, ndir, right_ref, left_ref, side_ref
        )


def step_kernel(first, side_first, last, *refs):
    (own_ref, pair_in, cross_in, side_in, speed_ref, lat_ref,
     shoal_ref, slope_x_ref, slope_y_ref, mask_ref, *refs) = refs
    if last:
        out_ref, new_ref, turn_ref, done_sem = refs[-4:]
    else:
        new_ref, right_ref, left_ref, side_ref, turn_ref = refs
    count, ndir = own_ref.shape[:2]
    quarter = ndir // 4
    row, lane = tile_ids()
    odd = (row & 1) == 1
    shoal = as_tile(shoal_ref)
    slope_x = as_tile(slope_x_ref)
    slope_y = as_tile(slope_y_ref)
    sea = as_tile(mask_ref)
    angle = [(d + 0.5) * (2.0 * math.pi / ndir) for d in range(ndir)]
    cos = [math.cos(a) for a in angle]
    sin = [math.sin(a) for a in angle]
    for d in range(ndir):
        turn_ref[d] = sin[d] * slope_x - cos[d] * slope_y

    odd_lon = lat_ref[4] == 1
    keep_up = lat_ref[2].astype(F32)
    keep_down = lat_ref[3].astype(F32)

    @pl.loop(0, count)
    def advance(f):
        speed = speed_ref[first + f]
        weight = shoal * speed
        up_all = side_in[lat_ref[0], side_first + f] * keep_up
        down_all = side_in[lat_ref[1], side_first + f] * keep_down

        def halved(d):
            field = own_ref[f, d]
            moved = weight * field
            if d >= 3 * quarter or d < quarter:
                edge = jnp.where(odd_lon, pair_in[f, d % quarter], cross_in[f, d % quarter])
                if d < quarter:
                    edge = pltpu.roll(edge, SUB - 1, 0)
                from_x = jnp.where(odd, pltpu.roll(moved, 1, 0), edge)
            else:
                edge = jnp.where(odd_lon, cross_in[f, d % quarter], pair_in[f, d % quarter])
                if d < 2 * quarter:
                    edge = pltpu.roll(edge, 1, 0)
                from_x = jnp.where(odd, edge, pltpu.roll(moved, SUB - 1, 0))
            if d < 2 * quarter:
                near = pltpu.roll(moved, 1, 1)
                edge = pltpu.roll(up_all, LANES - d, 1) if d else up_all
                far = pltpu.roll(jnp.where(row >= SUB - 2, edge, near), 2, 0)
                from_y = jnp.where(lane == 0, far, near)
            else:
                near = pltpu.roll(moved, LANES - 1, 1)
                edge = pltpu.roll(down_all, LANES - 1 - (d - 2 * quarter), 1)
                far = pltpu.roll(jnp.where(row < 2, edge, near), SUB - 2, 0)
                from_y = jnp.where(lane == LANES - 1, far, near)
            along, across = abs(cos[d]), abs(sin[d])
            half = field - (along + across) * moved + along * from_x + across * from_y
            return half, turn_ref[d] * (half * speed)

        half_top, qt_top = halved(ndir - 1)
        half, qt = halved(0)
        below = jnp.maximum(qt_top, 0.0) + jnp.minimum(qt, 0.0)
        flux_top = below
        for d in range(ndir):
            if d < ndir - 2:
                half_next, qt_next = halved(d + 1)
            else:
                half_next, qt_next = half_top, qt_top
            if d < ndir - 1:
                above = jnp.maximum(qt, 0.0) + jnp.minimum(qt_next, 0.0)
            else:
                above = flux_top
            new_ref[f, d] = (half - above + below) * sea
            half, qt, below = half_next, qt_next, above
        if not last:
            edge_messages(
                lambda d: new_ref[f, d], weight, odd_lon, f, ndir, right_ref, left_ref, side_ref
            )

    if last:
        copy = pltpu.make_async_copy(new_ref, out_ref.at[pl.ds(first, count)], done_sem)
        copy.start()
        copy.wait()


def params():
    return pltpu.CompilerParams(vmem_limit_bytes=VMEM_LIMIT)


def vmem(count):
    return [pl.BlockSpec(memory_space=pltpu.VMEM)] * count


SMEM_SPEC = pl.BlockSpec(memory_space=pltpu.SMEM)
ANY_SPEC = pl.BlockSpec(memory_space=pl.ANY)
HBM_SPEC = pl.BlockSpec(memory_space=pltpu.HBM)


def edge_shapes(count, ndir):
    tile = jax.ShapeDtypeStruct((count, ndir // 4, SUB, LANES), F32)
    line = jax.ShapeDtypeStruct((count, SUB, LANES), F32)
    return [tile, tile, line]


def send_edges(pair, cross):
    lon = lax.axis_size("lon")
    return (
        lax.ppermute(pair, "lon", [(i, i ^ 1) for i in range(lon)]),
        lax.ppermute(cross, "lon", [(i, (i + 2 * (i & 1) - 1) % lon) for i in range(lon)]),
    )


def on_device(spectra, wind_growth, wind_dir, point_cell, land_mask, shoaling, slope_x, slope_y):
    nfreq, ndir, slots = spectra.shape
    rows_x, rows_y = land_mask.shape
    lat_count = lax.axis_size("lat")
    devices = lax.axis_size("lon") * lat_count
    cap = slots // devices
    speed = jnp.asarray((0.65 * 1.1 ** -np.arange(nfreq)).astype(np.float32))
    starts = [sum(CHUNKS[:i]) for i in range(len(CHUNKS))]
    plans = [Plan(count, ndir, cap, i == 0) for i, count in enumerate(CHUNKS)]

    messages = []
    for i, (first, count, plan) in enumerate(zip(starts, CHUNKS, plans)):
        shape = jax.ShapeDtypeStruct((devices, plan.padded, LANES), F32)
        scratch = [
            pltpu.VMEM((plan.total, slots), F32),
            pltpu.VMEM((2 * plan.total, slots), BF16),
        ]
        if i == 0:
            message, gain, target = pl.pallas_call(
                functools.partial(
                    first_source_kernel, plan, count, (rows_x, rows_y, lat_count, devices)
                ),
                out_shape=[
                    shape,
                    jax.ShapeDtypeStruct((ndir, slots), F32),
                    jax.ShapeDtypeStruct((1, slots), jnp.int32),
                ],
                in_specs=[HBM_SPEC] * 4,
                out_specs=[HBM_SPEC] + vmem(2),
                scratch_shapes=[
                    pltpu.VMEM(spectra.shape, F32),
                    pltpu.VMEM((1, slots), F32),
                    pltpu.VMEM((1, slots), F32),
                    pltpu.VMEM((1, slots), jnp.int32),
                    *scratch,
                    pltpu.VMEM(shape.shape, F32),
                    pltpu.SemaphoreType.DMA((PIECES + 3,)),
                    pltpu.SemaphoreType.DMA((slots // NBLOCK,)),
                ],
                compiler_params=pltpu.CompilerParams(vmem_limit_bytes=60 * 2**20),
                name="source_first",
            )(
                spectra,
                wind_growth.reshape(1, slots),
                wind_dir.reshape(1, slots),
                point_cell.reshape(1, slots),
            )
        else:
            message = pl.pallas_call(
                functools.partial(later_source_kernel, plan, first, count, nfreq),
                out_shape=shape,
                in_specs=[pl.BlockSpec((pl.Element(count), pl.Element(ndir), pl.Element(slots)), lambda i, s=first: (s, 0, 0))]
                + [pl.BlockSpec((ndir, slots), lambda i: (0, 0)), pl.BlockSpec((1, slots), lambda i: (0, 0))],
                out_specs=pl.BlockSpec(shape.shape, lambda i: (0, 0, 0)),
                grid=(1,),
                scratch_shapes=scratch,
                compiler_params=params(),
                name="source_later",
            )(spectra, gain, target)
        messages.append(message)

    whole = jax.ShapeDtypeStruct((nfreq, ndir, SUB, LANES), F32)
    grids = (shoaling, slope_x, slope_y, land_mask)
    lat = lax.axis_index("lat")
    lat_ids = jnp.stack(
        [
            jnp.maximum(lat - 1, 0),
            jnp.minimum(lat + 1, lat_count - 1),
            (lat > 0).astype(jnp.int32),
            (lat < lat_count - 1).astype(jnp.int32),
            lax.axis_index("lon") & 1,
        ]
    )
    label = None
    out = None

    def place(i, arrived, after=()):
        first, count, plan = starts[i], CHUNKS[i], plans[i]
        outs = [jax.ShapeDtypeStruct((count * ndir * SUB, LANES), F32)] + edge_shapes(count, ndir)
        if i == 0:
            outs.append(jax.ShapeDtypeStruct((1, slots), jnp.int32))
        field, *sent = pl.pallas_call(
            functools.partial(place_kernel, plan, first, count, ndir, i == 0),
            out_shape=outs,
            in_specs=vmem(1) + [SMEM_SPEC, SMEM_SPEC] + vmem(1 if i == 0 else 2) + [ANY_SPEC] * len(after),
            out_specs=vmem(len(outs)),
            scratch_shapes=[
                pltpu.VMEM((plan.total, slots), F32),
                pltpu.VMEM((2 * plan.total, slots), BF16),
            ],
            compiler_params=params(),
            name="place",
        )(arrived, speed, lat_ids, shoaling, *([] if i == 0 else [label]), *after)
        return field.reshape(count, ndir, SUB, LANES), sent

    def step(i, field, received, side_first):
        same = jax.ShapeDtypeStruct(field.shape, F32)
        field, *sent = pl.pallas_call(
            functools.partial(step_kernel, starts[i], side_first, False),
            out_shape=[same] + edge_shapes(CHUNKS[i], ndir),
            in_specs=vmem(4) + [SMEM_SPEC, SMEM_SPEC] + vmem(4),
            out_specs=vmem(4),
            scratch_shapes=[pltpu.VMEM((ndir, SUB, LANES), F32)],
            compiler_params=params(),
            name="step",
        )(field, *received, speed, lat_ids, *grids)
        return field, sent

    def last_step(i, field, received, side_first, out, after=()):
        chained = out is not None
        return pl.pallas_call(
            functools.partial(step_kernel, starts[i], side_first, True),
            out_shape=whole,
            in_specs=vmem(4) + [SMEM_SPEC, SMEM_SPEC] + vmem(4) + [ANY_SPEC] * (len(after) + chained),
            out_specs=ANY_SPEC,
            scratch_shapes=[
                pltpu.VMEM(field.shape, F32),
                pltpu.VMEM((ndir, SUB, LANES), F32),
                pltpu.SemaphoreType.DMA(()),
            ],
            input_output_aliases={10: 0} if chained else {},
            compiler_params=params(),
            name="last_step",
        )(field, *received, speed, lat_ids, *grids, *([out] if chained else []), *after)

    n = len(CHUNKS)
    tie = lax.optimization_barrier
    waiting = None
    for i in range(n):
        arrived = lax.all_to_all(
            messages[i], ("lon", "lat"), split_axis=0, concat_axis=0, tiled=True
        )
        if i + 1 < n:
            arrived, messages[i + 1] = tie((arrived, messages[i + 1]))
        if i >= 2:
            arrived, out = tie((arrived, out))
        after = (waiting[2],) if i >= 2 else ()
        field, sent = place(i, arrived, after)
        if i == 0:
            *sent, label = sent
        received = send_edges(*sent[:2])
        if waiting is None:
            sides = lax.all_gather(sent[2], "lat")
            side_first = 0
        else:
            sides = lax.all_gather(jnp.concatenate([waiting[2], sent[2]], axis=0), "lat")
            side_first = CHUNKS[i - 1]
            if i < n - 1:
                out = last_step(i - 1, waiting[0], (*waiting[1], sides), 0, out)
            else:
                pending = (i - 1, waiting[0], (*waiting[1], sides), 0, out)
        field, sent = step(i, field, (*received, sides), side_first)
        if i + 2 < n:
            *sent, messages[i + 2] = tie((*sent, messages[i + 2]))
        waiting = (field, send_edges(*sent[:2]), sent[2])
    field, received, side = waiting
    sides = lax.all_gather(side, "lat")
    out = last_step(*pending, (sides,))
    out = last_step(n - 1, field, (*received, sides), 0, out)
    bands = rows_y // LANES
    out = out.reshape(nfreq, ndir, bands, rows_x, LANES)
    return out.transpose(0, 1, 3, 2, 4).reshape(nfreq, ndir, rows_x, rows_y)


def solution(mesh):
    placed = (
        P(None, None, ("lon", "lat")),
        P(("lon", "lat")),
        P(("lon", "lat")),
        P(("lon", "lat")),
        P("lon", "lat"),
        P("lon", "lat"),
        P("lon", "lat"),
        P("lon", "lat"),
    )
    return jax.shard_map(
        on_device,
        mesh=mesh,
        in_specs=placed,
        out_specs=P(None, None, "lon", "lat"),
        check_vma=False,
    )
```

```python
import functools
import math

import jax
import jax.numpy as jnp
import numpy as np
from jax import lax
from jax.experimental import pallas as pl
from jax.experimental.pallas import tpu as pltpu
from jax.sharding import PartitionSpec as P

F32 = jnp.float32
BF16 = jnp.bfloat16
LANES = 128
SUB = 8
CHUNKS = (9, 8, 8)
NBLOCK = 256
VMEM_LIMIT = 32 * 2**20


def ceil_to(value, step):
    return -(-value // step) * step


def divide(value, count):
    if count & (count - 1) == 0:
        return value >> (count.bit_length() - 1), value & (count - 1)
    quotient = value // count
    return quotient, value - quotient * count


class Plan:
    def __init__(self, count, ndir, cap, labels):
        self.cap = cap
        self.parts = LANES // cap
        self.rows = count * ndir + (1 if labels else 0)
        self.per = -(-self.rows // self.parts)
        self.padded = ceil_to(self.per, SUB)
        self.total = self.parts * self.padded
        self.label_row = (
            count * ndir // self.per * self.padded + count * ndir % self.per if labels else None
        )

    def pieces(self, start, length):
        found = []
        at = start
        while at < start + length:
            part, inside = divmod(at, self.per)
            take = min(self.per - inside, start + length - at)
            found.append((at - start, part * self.padded + inside, take))
            at += take
        return found


def swap_blocks(blocks, cap):
    parts = len(blocks)
    lane = lax.broadcasted_iota(jnp.int32, blocks[0].shape, 1)
    rolled = [pltpu.roll(b, cap * q, 1) if q else b for q, b in enumerate(blocks)]
    result = []
    for i in range(parts):
        mixed = rolled[-i % parts]
        for j in range(1, parts):
            mixed = jnp.where(lane >= j * cap, rolled[(j - i) % parts], mixed)
        result.append(pltpu.roll(mixed, LANES - cap * i, 1) if i else mixed)
    return result


def split_rows(x_ref, pair_ref):
    total = x_ref.shape[0]
    whole = x_ref[...]
    high = whole.astype(BF16)
    pair_ref[0:total, :] = high
    pair_ref[total : 2 * total, :] = (whole - high.astype(F32)).astype(BF16)


def route(pair_ref, picks, first):
    slots = pair_ref.shape[1]
    total = pair_ref.shape[0] // 2
    wanted = lax.broadcasted_iota(jnp.int32, (NBLOCK, slots), 0) + first
    onehot = jnp.where(wanted == picks, 1.0, 0.0).astype(BF16)
    both = lax.dot_general(
        pair_ref[...], onehot, (((1,), (1,)), ((), ())), preferred_element_type=F32
    )
    return both[:total] + both[total:]


def send_rows(plan, pair_ref, target, out_ref, done=None):
    slots = pair_ref.shape[1]
    groups = NBLOCK // LANES
    for block in range(slots // NBLOCK):
        moved = route(pair_ref, target, block * NBLOCK)
        for g in range(groups):
            blocks = [
                moved[q * plan.padded : (q + 1) * plan.padded, g * LANES : (g + 1) * LANES]
                for q in range(plan.parts)
            ]
            for i, message in enumerate(swap_blocks(blocks, plan.cap)):
                out_ref[(block * groups + g) * plan.parts + i] = message
        if done is not None:
            done(block)


def source_rows(plan, spectra_ref, first, count, nfreq, gain, x_ref):
    ndir = spectra_ref.shape[1]
    for f in range(count):
        ratio = float(np.float32(1.1) ** np.float32(first + f - (nfreq - 1)))
        rows = spectra_ref[f] * jnp.exp(gain * ratio)
        for offset, row, length in plan.pieces(f * ndir, ndir):
            x_ref[row : row + length, :] = rows[offset : offset + length]


PIECES = 5


def first_source_kernel(
    plan, count, shape, spectra_hbm, growth_hbm, dir_hbm, cell_hbm,
    out_hbm, gain_ref, target_ref,
    spectra_ref, growth_ref, dir_ref, cell_ref, x_ref, pair_ref, message_ref, sems, out_sems,
):
    rows_x, rows_y, lat_count, devices = shape
    nfreq, ndir, slots = spectra_ref.shape
    bounds = [nfreq * k // PIECES for k in range(PIECES + 1)]
    small = [
        pltpu.make_async_copy(src, dst, sems.at[PIECES + k])
        for k, (src, dst) in enumerate(
            ((cell_hbm, cell_ref), (growth_hbm, growth_ref), (dir_hbm, dir_ref))
        )
    ]
    pieces = [
        pltpu.make_async_copy(
            spectra_hbm.at[pl.ds(lo, hi - lo)], spectra_ref.at[pl.ds(lo, hi - lo)], sems.at[k]
        )
        for k, (lo, hi) in enumerate(zip(bounds, bounds[1:]))
    ]
    for copy in small + pieces:
        copy.start()
    small[0].wait()
    point = cell_ref[...]
    valid = point >= 0
    col_x, col_y = divide(jnp.maximum(point, 0), rows_y * lat_count)
    own_x, in_x = divide(col_x, rows_x)
    own_y, in_y = divide(col_y, rows_y)
    owner = jnp.where(valid, own_x * lat_count + own_y, devices)
    band, lane = divide(in_y, LANES)
    label = jnp.where(valid, (band * rows_x + in_x) * LANES + lane + 1, 0).astype(F32)
    ids = lax.broadcasted_iota(jnp.int32, (devices, slots), 0)
    hits = jnp.where(ids == owner, 1.0, 0.0)
    lower = lax.broadcasted_iota(jnp.int32, (LANES, LANES), 0) < lax.broadcasted_iota(
        jnp.int32, (LANES, LANES), 1
    )
    ahead = jnp.where(lower, 1.0, 0.0).astype(BF16)
    carry = jnp.zeros((devices, 1), F32)
    places = []
    for b in range(slots // LANES):
        part = hits[:, b * LANES : (b + 1) * LANES]
        before = jnp.dot(part.astype(BF16), ahead, preferred_element_type=F32) + carry
        places.append(jnp.sum(before * part, axis=0, keepdims=True))
        carry = carry + jnp.sum(part, axis=1, keepdims=True)
    place = jnp.concatenate(places, axis=1).astype(jnp.int32)
    target = jnp.where(valid, owner * plan.cap + place, slots)
    target_ref[...] = target

    small[1].wait()
    small[2].wait()
    dtheta = 2.0 * math.pi / ndir
    total = None
    for k, copy in enumerate(pieces):
        copy.wait()
        for f in range(bounds[k], bounds[k + 1]):
            width = float(np.float32(0.1) * np.float32(1.1) ** np.float32(f)) * dtheta
            term = spectra_ref[f] * width
            total = term if total is None else total + term
    energy = jnp.sum(total, axis=0, keepdims=True)
    load = energy / (energy + 10.0)
    theta = (lax.broadcasted_iota(jnp.int32, (ndir, slots), 0).astype(F32) + 0.5) * dtheta
    lobe = jnp.maximum(jnp.cos(theta - dir_ref[...]), 0.0)
    gain = growth_ref[...] * (lobe * lobe) - 0.4 * load
    gain_ref[...] = gain

    source_rows(plan, spectra_ref, 0, count, nfreq, gain, x_ref)
    x_ref[plan.label_row : plan.label_row + 1, :] = label
    split_rows(x_ref, pair_ref)
    copies = []

    def sent(block):
        per = devices * NBLOCK // slots
        part = pl.ds(block * per, per)
        copies.append(
            pltpu.make_async_copy(message_ref.at[part], out_hbm.at[part], out_sems.at[block])
        )
        copies[-1].start()

    send_rows(plan, pair_ref, target, message_ref, sent)
    for copy in copies:
        copy.wait()


def later_source_kernel(
    plan, first, count, nfreq, spectra_ref, gain_ref, target_ref, out_ref, x_ref, pair_ref
):
    source_rows(plan, spectra_ref, first, count, nfreq, gain_ref[...], x_ref)
    split_rows(x_ref, pair_ref)
    send_rows(plan, pair_ref, target_ref[...], out_ref)


def as_tile(grid_ref):
    grid = grid_ref[...].astype(F32)
    bands = grid.shape[1] // LANES
    return jnp.concatenate([grid[:, b * LANES : (b + 1) * LANES] for b in range(bands)], axis=0)


def tile_ids():
    return (
        lax.broadcasted_iota(jnp.int32, (SUB, LANES), 0),
        lax.broadcasted_iota(jnp.int32, (SUB, LANES), 1),
    )


def edge_messages(read, weight, odd_lon, f, ndir, near_ref, cross_ref, side_ref):
    row, lane = tile_ids()
    odd = (row & 1) == 1
    quarter = ndir // 4
    up = jnp.zeros((SUB, LANES), F32)
    down = jnp.zeros((SUB, LANES), F32)
    moved = [read(d) * weight for d in range(ndir)]
    for e in range(quarter):
        a, b = moved[3 * quarter + e], moved[e]
        right = jnp.where(odd, b, pltpu.roll(a, SUB - 1, 0))
        a, b = moved[quarter + e], moved[2 * quarter + e]
        left = jnp.where(odd, pltpu.roll(b, 1, 0), a)
        near_ref[f, e] = jnp.where(odd_lon, left, right)
        cross_ref[f, e] = jnp.where(odd_lon, right, left)
    for k in range(2 * quarter):
        up = jnp.where(lane == k, pltpu.roll(moved[k], k + 1, 1), up)
        low = moved[2 * quarter + k]
        down = jnp.where(lane == k, pltpu.roll(low, k, 1) if k else low, down)
    side_ref[f] = jnp.where(row >= SUB // 2, up, down)


def place_kernel(plan, first, count, ndir, with_labels, *refs):
    if with_labels:
        in_ref, speed_ref, ids_ref, shoal_ref, *refs = refs
        own_ref, near_ref, cross_ref, side_ref, label_ref, x_ref, pair_ref = refs
    else:
        in_ref, speed_ref, ids_ref, shoal_ref, label_ref, *refs = refs
        refs = refs[-6:]
        own_ref, near_ref, cross_ref, side_ref, x_ref, pair_ref = refs
    slots = x_ref.shape[1]
    for g in range(slots // LANES):
        blocks = [in_ref[g * plan.parts + i] for i in range(plan.parts)]
        for q, part in enumerate(swap_blocks(blocks, plan.cap)):
            x_ref[q * plan.padded : (q + 1) * plan.padded, g * LANES : (g + 1) * LANES] = part
    if with_labels:
        label_ref[...] = x_ref[plan.label_row : plan.label_row + 1, :].astype(jnp.int32) - 1
    label = label_ref[...]
    split_rows(x_ref, pair_ref)
    for block in range(slots // NBLOCK):
        placed = route(pair_ref, label, block * NBLOCK)
        for t in range(NBLOCK // LANES):
            row = block * (NBLOCK // LANES) + t
            for q in range(plan.parts):
                length = min(plan.per, count * ndir - q * plan.per)
                if length > 0:
                    own_ref[pl.ds(q * plan.per * SUB + row, length, stride=SUB), :] = placed[
                        q * plan.padded : q * plan.padded + length, t * LANES : (t + 1) * LANES
                    ]
    shoal = as_tile(shoal_ref)

    @pl.loop(0, count)
    def pack(f):
        def read(d):
            return own_ref[pl.ds(pl.multiple_of((f * ndir + d) * SUB, SUB), SUB), :]

        edge_messages(
            read, shoal * speed_ref[first + f], ids_ref[4] == 1, f, ndir, near_ref, cross_ref, side_ref
        )


def step_kernel(first, side_first, last, *refs):
    (own_ref, pair_in, cross_in, side_in, speed_ref, lat_ref,
     shoal_ref, slope_x_ref, slope_y_ref, mask_ref, *refs) = refs
    if last:
        out_ref, new_ref, turn_ref, done_sem = refs[-4:]
    else:
        new_ref, near_ref, cross_ref, side_ref, turn_ref = refs
    count, ndir = own_ref.shape[:2]
    quarter = ndir // 4
    row, lane = tile_ids()
    odd = (row & 1) == 1
    shoal = as_tile(shoal_ref)
    slope_x = as_tile(slope_x_ref)
    slope_y = as_tile(slope_y_ref)
    sea = as_tile(mask_ref)
    angle = [(d + 0.5) * (2.0 * math.pi / ndir) for d in range(ndir)]
    cos = [math.cos(a) for a in angle]
    sin = [math.sin(a) for a in angle]
    for d in range(ndir):
        turn_ref[d] = sin[d] * slope_x - cos[d] * slope_y

    odd_lon = lat_ref[4] == 1
    keep_up = lat_ref[2].astype(F32)
    keep_down = lat_ref[3].astype(F32)

    def write(f):
        return pltpu.make_async_copy(new_ref.at[f], out_ref.at[first + f], done_sem.at[f])

    @pl.loop(0, count)
    def advance(f):
        speed = speed_ref[first + f]
        weight = shoal * speed
        up_all = side_in[lat_ref[0], side_first + f] * keep_up
        down_all = side_in[lat_ref[1], side_first + f] * keep_down

        def halved(d):
            field = own_ref[f, d]
            moved = weight * field
            if d >= 3 * quarter or d < quarter:
                edge = jnp.where(odd_lon, pair_in[f, d % quarter], cross_in[f, d % quarter])
                if d < quarter:
                    edge = pltpu.roll(edge, SUB - 1, 0)
                from_x = jnp.where(odd, pltpu.roll(moved, 1, 0), edge)
            else:
                edge = jnp.where(odd_lon, cross_in[f, d % quarter], pair_in[f, d % quarter])
                if d < 2 * quarter:
                    edge = pltpu.roll(edge, 1, 0)
                from_x = jnp.where(odd, edge, pltpu.roll(moved, SUB - 1, 0))
            if d < 2 * quarter:
                near = pltpu.roll(moved, 1, 1)
                edge = pltpu.roll(up_all, LANES - d, 1) if d else up_all
                far = pltpu.roll(jnp.where(row >= SUB - 2, edge, near), 2, 0)
                from_y = jnp.where(lane == 0, far, near)
            else:
                near = pltpu.roll(moved, LANES - 1, 1)
                edge = pltpu.roll(down_all, LANES - 1 - (d - 2 * quarter), 1)
                far = pltpu.roll(jnp.where(row < 2, edge, near), SUB - 2, 0)
                from_y = jnp.where(lane == LANES - 1, far, near)
            along, across = abs(cos[d]), abs(sin[d])
            half = field - (along + across) * moved + along * from_x + across * from_y
            return half, turn_ref[d] * (half * speed)

        half_top, qt_top = halved(ndir - 1)
        half, qt = halved(0)
        below = jnp.maximum(qt_top, 0.0) + jnp.minimum(qt, 0.0)
        flux_top = below
        for d in range(ndir):
            if d < ndir - 2:
                half_next, qt_next = halved(d + 1)
            else:
                half_next, qt_next = half_top, qt_top
            if d < ndir - 1:
                above = jnp.maximum(qt, 0.0) + jnp.minimum(qt_next, 0.0)
            else:
                above = flux_top
            new_ref[f, d] = (half - above + below) * sea
            half, qt, below = half_next, qt_next, above
        if not last:
            edge_messages(
                lambda d: new_ref[f, d], weight, odd_lon, f, ndir, near_ref, cross_ref, side_ref
            )
        if last:
            write(f).start()

    if last:

        @pl.loop(0, count)
        def finish(f):
            write(f).wait()


def params():
    return pltpu.CompilerParams(vmem_limit_bytes=VMEM_LIMIT)


def vmem(count):
    return [pl.BlockSpec(memory_space=pltpu.VMEM)] * count


SMEM_SPEC = pl.BlockSpec(memory_space=pltpu.SMEM)
ANY_SPEC = pl.BlockSpec(memory_space=pl.ANY)
HBM_SPEC = pl.BlockSpec(memory_space=pltpu.HBM)


def edge_shapes(count, ndir):
    tile = jax.ShapeDtypeStruct((count, ndir // 4, SUB, LANES), F32)
    line = jax.ShapeDtypeStruct((count, SUB, LANES), F32)
    return [tile, tile, line]


def send_edges(pair, cross):
    lon = lax.axis_size("lon")
    return (
        lax.ppermute(pair, "lon", [(i, i ^ 1) for i in range(lon)]),
        lax.ppermute(cross, "lon", [(i, (i + 2 * (i & 1) - 1) % lon) for i in range(lon)]),
    )


def on_device(spectra, wind_growth, wind_dir, point_cell, land_mask, shoaling, slope_x, slope_y):
    nfreq, ndir, slots = spectra.shape
    rows_x, rows_y = land_mask.shape
    lat_count = lax.axis_size("lat")
    devices = lax.axis_size("lon") * lat_count
    cap = slots // devices
    speed = jnp.asarray((0.65 * 1.1 ** -np.arange(nfreq)).astype(np.float32))
    starts = [sum(CHUNKS[:i]) for i in range(len(CHUNKS))]
    plans = [Plan(count, ndir, cap, i == 0) for i, count in enumerate(CHUNKS)]

    messages = []
    for i, (first, count, plan) in enumerate(zip(starts, CHUNKS, plans)):
        shape = jax.ShapeDtypeStruct((devices, plan.padded, LANES), F32)
        scratch = [
            pltpu.VMEM((plan.total, slots), F32),
            pltpu.VMEM((2 * plan.total, slots), BF16),
        ]
        if i == 0:
            message, gain, target = pl.pallas_call(
                functools.partial(
                    first_source_kernel, plan, count, (rows_x, rows_y, lat_count, devices)
                ),
                out_shape=[
                    shape,
                    jax.ShapeDtypeStruct((ndir, slots), F32),
                    jax.ShapeDtypeStruct((1, slots), jnp.int32),
                ],
                in_specs=[HBM_SPEC] * 4,
                out_specs=[HBM_SPEC] + vmem(2),
                scratch_shapes=[
                    pltpu.VMEM(spectra.shape, F32),
                    pltpu.VMEM((1, slots), F32),
                    pltpu.VMEM((1, slots), F32),
                    pltpu.VMEM((1, slots), jnp.int32),
                    *scratch,
                    pltpu.VMEM(shape.shape, F32),
                    pltpu.SemaphoreType.DMA((PIECES + 3,)),
                    pltpu.SemaphoreType.DMA((slots // NBLOCK,)),
                ],
                compiler_params=pltpu.CompilerParams(vmem_limit_bytes=60 * 2**20),
                name="source_first",
            )(
                spectra,
                wind_growth.reshape(1, slots),
                wind_dir.reshape(1, slots),
                point_cell.reshape(1, slots),
            )
        else:
            message = pl.pallas_call(
                functools.partial(later_source_kernel, plan, first, count, nfreq),
                out_shape=shape,
                in_specs=[pl.BlockSpec((pl.Element(count), pl.Element(ndir), pl.Element(slots)), lambda i, s=first: (s, 0, 0))]
                + [pl.BlockSpec((ndir, slots), lambda i: (0, 0)), pl.BlockSpec((1, slots), lambda i: (0, 0))],
                out_specs=pl.BlockSpec(shape.shape, lambda i: (0, 0, 0)),
                grid=(1,),
                scratch_shapes=scratch,
                compiler_params=params(),
                name="source_later",
            )(spectra, gain, target)
        messages.append(message)

    whole = jax.ShapeDtypeStruct((nfreq, ndir, SUB, LANES), F32)
    grids = (shoaling, slope_x, slope_y, land_mask)
    lat = lax.axis_index("lat")
    lat_ids = jnp.stack(
        [
            jnp.maximum(lat - 1, 0),
            jnp.minimum(lat + 1, lat_count - 1),
            (lat > 0).astype(jnp.int32),
            (lat < lat_count - 1).astype(jnp.int32),
            lax.axis_index("lon") & 1,
        ]
    )
    label = None
    out = None

    def place(i, arrived, after=()):
        first, count, plan = starts[i], CHUNKS[i], plans[i]
        outs = [jax.ShapeDtypeStruct((count * ndir * SUB, LANES), F32)] + edge_shapes(count, ndir)
        if i == 0:
            outs.append(jax.ShapeDtypeStruct((1, slots), jnp.int32))
        field, *sent = pl.pallas_call(
            functools.partial(place_kernel, plan, first, count, ndir, i == 0),
            out_shape=outs,
            in_specs=vmem(1) + [SMEM_SPEC, SMEM_SPEC] + vmem(1 if i == 0 else 2) + [ANY_SPEC] * len(after),
            out_specs=vmem(len(outs)),
            scratch_shapes=[
                pltpu.VMEM((plan.total, slots), F32),
                pltpu.VMEM((2 * plan.total, slots), BF16),
            ],
            compiler_params=params(),
            name="place",
        )(arrived, speed, lat_ids, shoaling, *([] if i == 0 else [label]), *after)
        return field.reshape(count, ndir, SUB, LANES), sent

    def step(i, field, received, side_first):
        same = jax.ShapeDtypeStruct(field.shape, F32)
        field, *sent = pl.pallas_call(
            functools.partial(step_kernel, starts[i], side_first, False),
            out_shape=[same] + edge_shapes(CHUNKS[i], ndir),
            in_specs=vmem(4) + [SMEM_SPEC, SMEM_SPEC] + vmem(4),
            out_specs=vmem(4),
            scratch_shapes=[pltpu.VMEM((ndir, SUB, LANES), F32)],
            compiler_params=params(),
            name="step",
        )(field, *received, speed, lat_ids, *grids)
        return field, sent

    def last_step(i, field, received, side_first, out, after=()):
        chained = out is not None
        return pl.pallas_call(
            functools.partial(step_kernel, starts[i], side_first, True),
            out_shape=whole,
            in_specs=vmem(4) + [SMEM_SPEC, SMEM_SPEC] + vmem(4) + [ANY_SPEC] * (len(after) + chained),
            out_specs=ANY_SPEC,
            scratch_shapes=[
                pltpu.VMEM(field.shape, F32),
                pltpu.VMEM((ndir, SUB, LANES), F32),
                pltpu.SemaphoreType.DMA((CHUNKS[i],)),
            ],
            input_output_aliases={10: 0} if chained else {},
            compiler_params=params(),
            name="last_step",
        )(field, *received, speed, lat_ids, *grids, *([out] if chained else []), *after)

    n = len(CHUNKS)
    tie = lax.optimization_barrier
    waiting = None
    for i in range(n):
        arrived = lax.all_to_all(
            messages[i], ("lon", "lat"), split_axis=0, concat_axis=0, tiled=True
        )
        if i + 1 < n:
            arrived, messages[i + 1] = tie((arrived, messages[i + 1]))
        if i >= 2:
            arrived, out = tie((arrived, out))
        after = (waiting[2],) if i >= 2 else ()
        field, sent = place(i, arrived, after)
        if i == 0:
            *sent, label = sent
        received = send_edges(*sent[:2])
        if waiting is None:
            sides = lax.all_gather(sent[2], "lat")
            side_first = 0
        else:
            sides = lax.all_gather(jnp.concatenate([waiting[2], sent[2]], axis=0), "lat")
            side_first = CHUNKS[i - 1]
            if i < n - 1:
                out = last_step(i - 1, waiting[0], (*waiting[1], sides), 0, out)
            else:
                pending = (i - 1, waiting[0], (*waiting[1], sides), 0, out)
        field, sent = step(i, field, (*received, sides), side_first)
        if i + 2 < n:
            *sent, messages[i + 2] = tie((*sent, messages[i + 2]))
        waiting = (field, send_edges(*sent[:2]), sent[2])
    field, received, side = waiting
    sides = lax.all_gather(side, "lat")
    out = last_step(*pending, (sides,))
    out = last_step(n - 1, field, (*received, sides), 0, out)
    bands = rows_y // LANES
    out = out.reshape(nfreq, ndir, bands, rows_x, LANES)
    return out.transpose(0, 1, 3, 2, 4).reshape(nfreq, ndir, rows_x, rows_y)


def solution(mesh):
    placed = (
        P(None, None, ("lon", "lat")),
        P(("lon", "lat")),
        P(("lon", "lat")),
        P(("lon", "lat")),
        P("lon", "lat"),
        P("lon", "lat"),
        P("lon", "lat"),
        P("lon", "lat"),
    )
    return jax.shard_map(
        on_device,
        mesh=mesh,
        in_specs=placed,
        out_specs=P(None, None, "lon", "lat"),
        check_vma=False,
    )
```

```python
import functools
import math

import jax
import jax.numpy as jnp
import numpy as np
from jax import lax
from jax.experimental import pallas as pl
from jax.experimental.pallas import tpu as pltpu
from jax.sharding import PartitionSpec as P

F32 = jnp.float32
BF16 = jnp.bfloat16
LANES = 128
SUB = 8
CHUNKS = (10, 8, 7)
NBLOCK = 256
VMEM_LIMIT = 32 * 2**20


def ceil_to(value, step):
    return -(-value // step) * step


def divide(value, count):
    if count & (count - 1) == 0:
        return value >> (count.bit_length() - 1), value & (count - 1)
    quotient = value // count
    return quotient, value - quotient * count


class Plan:
    def __init__(self, count, ndir, cap, labels):
        self.cap = cap
        self.parts = LANES // cap
        self.rows = count * ndir + (1 if labels else 0)
        self.per = -(-self.rows // self.parts)
        self.padded = ceil_to(self.per, SUB)
        self.total = self.parts * self.padded
        self.label_row = (
            count * ndir // self.per * self.padded + count * ndir % self.per if labels else None
        )

    def pieces(self, start, length):
        found = []
        at = start
        while at < start + length:
            part, inside = divmod(at, self.per)
            take = min(self.per - inside, start + length - at)
            found.append((at - start, part * self.padded + inside, take))
            at += take
        return found


def swap_blocks(blocks, cap):
    parts = len(blocks)
    lane = lax.broadcasted_iota(jnp.int32, blocks[0].shape, 1)
    rolled = [pltpu.roll(b, cap * q, 1) if q else b for q, b in enumerate(blocks)]
    result = []
    for i in range(parts):
        mixed = rolled[-i % parts]
        for j in range(1, parts):
            mixed = jnp.where(lane >= j * cap, rolled[(j - i) % parts], mixed)
        result.append(pltpu.roll(mixed, LANES - cap * i, 1) if i else mixed)
    return result


def split_rows(x_ref, pair_ref):
    total = x_ref.shape[0]
    whole = x_ref[...]
    high = whole.astype(BF16)
    pair_ref[0:total, :] = high
    pair_ref[total : 2 * total, :] = (whole - high.astype(F32)).astype(BF16)


def route(pair_ref, picks, first):
    slots = pair_ref.shape[1]
    total = pair_ref.shape[0] // 2
    wanted = lax.broadcasted_iota(jnp.int32, (NBLOCK, slots), 0) + first
    onehot = jnp.where(wanted == picks, 1.0, 0.0).astype(BF16)
    both = lax.dot_general(
        pair_ref[...], onehot, (((1,), (1,)), ((), ())), preferred_element_type=F32
    )
    return both[:total] + both[total:]


def send_rows(plan, pair_ref, target, out_ref, done=None):
    slots = pair_ref.shape[1]
    groups = NBLOCK // LANES
    for block in range(slots // NBLOCK):
        moved = route(pair_ref, target, block * NBLOCK)
        for g in range(groups):
            blocks = [
                moved[q * plan.padded : (q + 1) * plan.padded, g * LANES : (g + 1) * LANES]
                for q in range(plan.parts)
            ]
            for i, message in enumerate(swap_blocks(blocks, plan.cap)):
                out_ref[(block * groups + g) * plan.parts + i] = message
        if done is not None:
            done(block)


def source_rows(plan, spectra_ref, first, count, nfreq, gain, x_ref):
    ndir = spectra_ref.shape[1]
    for f in range(count):
        ratio = float(np.float32(1.1) ** np.float32(first + f - (nfreq - 1)))
        rows = spectra_ref[f] * jnp.exp(gain * ratio)
        for offset, row, length in plan.pieces(f * ndir, ndir):
            x_ref[row : row + length, :] = rows[offset : offset + length]


PIECES = 5


def first_source_kernel(
    plan, count, shape, spectra_hbm, growth_hbm, dir_hbm, cell_hbm,
    out_hbm, gain_ref, target_ref,
    spectra_ref, growth_ref, dir_ref, cell_ref, x_ref, pair_ref, message_ref, sems, out_sems,
):
    rows_x, rows_y, lat_count, devices = shape
    nfreq, ndir, slots = spectra_ref.shape
    bounds = [nfreq * k // PIECES for k in range(PIECES + 1)]
    small = [
        pltpu.make_async_copy(src, dst, sems.at[PIECES + k])
        for k, (src, dst) in enumerate(
            ((cell_hbm, cell_ref), (growth_hbm, growth_ref), (dir_hbm, dir_ref))
        )
    ]
    pieces = [
        pltpu.make_async_copy(
            spectra_hbm.at[pl.ds(lo, hi - lo)], spectra_ref.at[pl.ds(lo, hi - lo)], sems.at[k]
        )
        for k, (lo, hi) in enumerate(zip(bounds, bounds[1:]))
    ]
    for copy in small + pieces:
        copy.start()
    small[0].wait()
    point = cell_ref[...]
    valid = point >= 0
    col_x, col_y = divide(jnp.maximum(point, 0), rows_y * lat_count)
    own_x, in_x = divide(col_x, rows_x)
    own_y, in_y = divide(col_y, rows_y)
    owner = jnp.where(valid, own_x * lat_count + own_y, devices)
    band, lane = divide(in_y, LANES)
    label = jnp.where(valid, (band * rows_x + in_x) * LANES + lane + 1, 0).astype(F32)
    ids = lax.broadcasted_iota(jnp.int32, (devices, slots), 0)
    hits = jnp.where(ids == owner, 1.0, 0.0)
    lower = lax.broadcasted_iota(jnp.int32, (LANES, LANES), 0) < lax.broadcasted_iota(
        jnp.int32, (LANES, LANES), 1
    )
    ahead = jnp.where(lower, 1.0, 0.0).astype(BF16)
    carry = jnp.zeros((devices, 1), F32)
    places = []
    for b in range(slots // LANES):
        part = hits[:, b * LANES : (b + 1) * LANES]
        before = jnp.dot(part.astype(BF16), ahead, preferred_element_type=F32) + carry
        places.append(jnp.sum(before * part, axis=0, keepdims=True))
        carry = carry + jnp.sum(part, axis=1, keepdims=True)
    place = jnp.concatenate(places, axis=1).astype(jnp.int32)
    target = jnp.where(valid, owner * plan.cap + place, slots)
    target_ref[...] = target

    small[1].wait()
    small[2].wait()
    dtheta = 2.0 * math.pi / ndir
    total = None
    for k, copy in enumerate(pieces):
        copy.wait()
        for f in range(bounds[k], bounds[k + 1]):
            width = float(np.float32(0.1) * np.float32(1.1) ** np.float32(f)) * dtheta
            term = spectra_ref[f] * width
            total = term if total is None else total + term
    energy = jnp.sum(total, axis=0, keepdims=True)
    load = energy / (energy + 10.0)
    theta = (lax.broadcasted_iota(jnp.int32, (ndir, slots), 0).astype(F32) + 0.5) * dtheta
    lobe = jnp.maximum(jnp.cos(theta - dir_ref[...]), 0.0)
    gain = growth_ref[...] * (lobe * lobe) - 0.4 * load
    gain_ref[...] = gain

    source_rows(plan, spectra_ref, 0, count, nfreq, gain, x_ref)
    x_ref[plan.label_row : plan.label_row + 1, :] = label
    split_rows(x_ref, pair_ref)
    copies = []

    def sent(block):
        per = devices * NBLOCK // slots
        part = pl.ds(block * per, per)
        copies.append(
            pltpu.make_async_copy(message_ref.at[part], out_hbm.at[part], out_sems.at[block])
        )
        copies[-1].start()

    send_rows(plan, pair_ref, target, message_ref, sent)
    for copy in copies:
        copy.wait()


def later_source_kernel(
    plan, first, count, nfreq, spectra_ref, gain_ref, target_ref, out_ref, x_ref, pair_ref
):
    source_rows(plan, spectra_ref, first, count, nfreq, gain_ref[...], x_ref)
    split_rows(x_ref, pair_ref)
    send_rows(plan, pair_ref, target_ref[...], out_ref)


def as_tile(grid_ref):
    grid = grid_ref[...].astype(F32)
    bands = grid.shape[1] // LANES
    return jnp.concatenate([grid[:, b * LANES : (b + 1) * LANES] for b in range(bands)], axis=0)


def tile_ids():
    return (
        lax.broadcasted_iota(jnp.int32, (SUB, LANES), 0),
        lax.broadcasted_iota(jnp.int32, (SUB, LANES), 1),
    )


def edge_messages(read, weight, odd_lon, f, ndir, near_ref, cross_ref, side_ref):
    row, lane = tile_ids()
    odd = (row & 1) == 1
    quarter = ndir // 4
    up = jnp.zeros((SUB, LANES), F32)
    down = jnp.zeros((SUB, LANES), F32)
    moved = [read(d) * weight for d in range(ndir)]
    for e in range(quarter):
        a, b = moved[3 * quarter + e], moved[e]
        right = jnp.where(odd, b, pltpu.roll(a, SUB - 1, 0))
        a, b = moved[quarter + e], moved[2 * quarter + e]
        left = jnp.where(odd, pltpu.roll(b, 1, 0), a)
        near_ref[f, e] = jnp.where(odd_lon, left, right)
        cross_ref[f, e] = jnp.where(odd_lon, right, left)
    for k in range(2 * quarter):
        up = jnp.where(lane == k, pltpu.roll(moved[k], k + 1, 1), up)
        low = moved[2 * quarter + k]
        down = jnp.where(lane == k, pltpu.roll(low, k, 1) if k else low, down)
    side_ref[f] = jnp.where(row >= SUB // 2, up, down)


def place_kernel(plan, first, count, ndir, with_labels, *refs):
    if with_labels:
        in_ref, speed_ref, ids_ref, shoal_ref, *refs = refs
        own_ref, near_ref, cross_ref, side_ref, label_ref, x_ref, pair_ref = refs
    else:
        in_ref, speed_ref, ids_ref, shoal_ref, label_ref, *refs = refs
        own_ref, near_ref, cross_ref, side_ref, x_ref, pair_ref = refs
    slots = x_ref.shape[1]
    for g in range(slots // LANES):
        blocks = [in_ref[g * plan.parts + i] for i in range(plan.parts)]
        for q, part in enumerate(swap_blocks(blocks, plan.cap)):
            x_ref[q * plan.padded : (q + 1) * plan.padded, g * LANES : (g + 1) * LANES] = part
    if with_labels:
        label_ref[...] = x_ref[plan.label_row : plan.label_row + 1, :].astype(jnp.int32) - 1
    label = label_ref[...]
    split_rows(x_ref, pair_ref)
    for block in range(slots // NBLOCK):
        placed = route(pair_ref, label, block * NBLOCK)
        for t in range(NBLOCK // LANES):
            row = block * (NBLOCK // LANES) + t
            for q in range(plan.parts):
                length = min(plan.per, count * ndir - q * plan.per)
                if length > 0:
                    own_ref[pl.ds(q * plan.per * SUB + row, length, stride=SUB), :] = placed[
                        q * plan.padded : q * plan.padded + length, t * LANES : (t + 1) * LANES
                    ]
    shoal = as_tile(shoal_ref)

    @pl.loop(0, count)
    def pack(f):
        def read(d):
            return own_ref[pl.ds(pl.multiple_of((f * ndir + d) * SUB, SUB), SUB), :]

        edge_messages(
            read, shoal * speed_ref[first + f], ids_ref[4] == 1, f, ndir, near_ref, cross_ref, side_ref
        )


def step_kernel(first, side_first, last, *refs):
    (own_ref, pair_in, cross_in, side_in, speed_ref, lat_ref,
     shoal_ref, slope_x_ref, slope_y_ref, mask_ref, *refs) = refs
    if last:
        out_ref, new_ref, turn_ref, done_sem = refs[-4:]
    else:
        new_ref, near_ref, cross_ref, side_ref, turn_ref = refs
    count, ndir = own_ref.shape[:2]
    quarter = ndir // 4
    row, lane = tile_ids()
    odd = (row & 1) == 1
    shoal = as_tile(shoal_ref)
    slope_x = as_tile(slope_x_ref)
    slope_y = as_tile(slope_y_ref)
    sea = as_tile(mask_ref)
    angle = [(d + 0.5) * (2.0 * math.pi / ndir) for d in range(ndir)]
    cos = [math.cos(a) for a in angle]
    sin = [math.sin(a) for a in angle]
    for d in range(ndir):
        turn_ref[d] = sin[d] * slope_x - cos[d] * slope_y

    odd_lon = lat_ref[4] == 1
    keep_up = lat_ref[2].astype(F32)
    keep_down = lat_ref[3].astype(F32)

    def write(f):
        return pltpu.make_async_copy(new_ref.at[f], out_ref.at[first + f], done_sem.at[f])

    @pl.loop(0, count)
    def advance(f):
        speed = speed_ref[first + f]
        weight = shoal * speed
        up_all = side_in[lat_ref[0], side_first + f] * keep_up
        down_all = side_in[lat_ref[1], side_first + f] * keep_down

        def halved(d):
            field = own_ref[f, d]
            moved = weight * field
            if d >= 3 * quarter or d < quarter:
                edge = jnp.where(odd_lon, pair_in[f, d % quarter], cross_in[f, d % quarter])
                if d < quarter:
                    edge = pltpu.roll(edge, SUB - 1, 0)
                from_x = jnp.where(odd, pltpu.roll(moved, 1, 0), edge)
            else:
                edge = jnp.where(odd_lon, cross_in[f, d % quarter], pair_in[f, d % quarter])
                if d < 2 * quarter:
                    edge = pltpu.roll(edge, 1, 0)
                from_x = jnp.where(odd, edge, pltpu.roll(moved, SUB - 1, 0))
            if d < 2 * quarter:
                near = pltpu.roll(moved, 1, 1)
                edge = pltpu.roll(up_all, LANES - d, 1) if d else up_all
                far = pltpu.roll(jnp.where(row >= SUB - 2, edge, near), 2, 0)
                from_y = jnp.where(lane == 0, far, near)
            else:
                near = pltpu.roll(moved, LANES - 1, 1)
                edge = pltpu.roll(down_all, LANES - 1 - (d - 2 * quarter), 1)
                far = pltpu.roll(jnp.where(row < 2, edge, near), SUB - 2, 0)
                from_y = jnp.where(lane == LANES - 1, far, near)
            along, across = abs(cos[d]), abs(sin[d])
            half = field - (along + across) * moved + along * from_x + across * from_y
            return half, turn_ref[d] * (half * speed)

        half_top, qt_top = halved(ndir - 1)
        half, qt = halved(0)
        below = jnp.maximum(qt_top, 0.0) + jnp.minimum(qt, 0.0)
        flux_top = below
        for d in range(ndir):
            if d < ndir - 2:
                half_next, qt_next = halved(d + 1)
            else:
                half_next, qt_next = half_top, qt_top
            if d < ndir - 1:
                above = jnp.maximum(qt, 0.0) + jnp.minimum(qt_next, 0.0)
            else:
                above = flux_top
            new_ref[f, d] = (half - above + below) * sea
            half, qt, below = half_next, qt_next, above
        if not last:
            edge_messages(
                lambda d: new_ref[f, d], weight, odd_lon, f, ndir, near_ref, cross_ref, side_ref
            )
        if last:
            write(f).start()

    if last:

        @pl.loop(0, count)
        def finish(f):
            write(f).wait()


def params():
    return pltpu.CompilerParams(vmem_limit_bytes=VMEM_LIMIT)


def vmem(count):
    return [pl.BlockSpec(memory_space=pltpu.VMEM)] * count


SMEM_SPEC = pl.BlockSpec(memory_space=pltpu.SMEM)
ANY_SPEC = pl.BlockSpec(memory_space=pl.ANY)
HBM_SPEC = pl.BlockSpec(memory_space=pltpu.HBM)


def edge_shapes(count, ndir):
    tile = jax.ShapeDtypeStruct((count, ndir // 4, SUB, LANES), F32)
    line = jax.ShapeDtypeStruct((count, SUB, LANES), F32)
    return [tile, tile, line]


def send_edges(pair, cross):
    lon = lax.axis_size("lon")
    return (
        lax.ppermute(pair, "lon", [(i, i ^ 1) for i in range(lon)]),
        lax.ppermute(cross, "lon", [(i, (i + 2 * (i & 1) - 1) % lon) for i in range(lon)]),
    )


def on_device(spectra, wind_growth, wind_dir, point_cell, land_mask, shoaling, slope_x, slope_y):
    nfreq, ndir, slots = spectra.shape
    rows_x, rows_y = land_mask.shape
    lat_count = lax.axis_size("lat")
    devices = lax.axis_size("lon") * lat_count
    cap = slots // devices
    speed = jnp.asarray((0.65 * 1.1 ** -np.arange(nfreq)).astype(np.float32))
    starts = [sum(CHUNKS[:i]) for i in range(len(CHUNKS))]
    plans = [Plan(count, ndir, cap, i == 0) for i, count in enumerate(CHUNKS)]

    messages = []
    for i, (first, count, plan) in enumerate(zip(starts, CHUNKS, plans)):
        shape = jax.ShapeDtypeStruct((devices, plan.padded, LANES), F32)
        scratch = [
            pltpu.VMEM((plan.total, slots), F32),
            pltpu.VMEM((2 * plan.total, slots), BF16),
        ]
        if i == 0:
            message, gain, target = pl.pallas_call(
                functools.partial(
                    first_source_kernel, plan, count, (rows_x, rows_y, lat_count, devices)
                ),
                out_shape=[
                    shape,
                    jax.ShapeDtypeStruct((ndir, slots), F32),
                    jax.ShapeDtypeStruct((1, slots), jnp.int32),
                ],
                in_specs=[HBM_SPEC] * 4,
                out_specs=[HBM_SPEC] + vmem(2),
                scratch_shapes=[
                    pltpu.VMEM(spectra.shape, F32),
                    pltpu.VMEM((1, slots), F32),
                    pltpu.VMEM((1, slots), F32),
                    pltpu.VMEM((1, slots), jnp.int32),
                    *scratch,
                    pltpu.VMEM(shape.shape, F32),
                    pltpu.SemaphoreType.DMA((PIECES + 3,)),
                    pltpu.SemaphoreType.DMA((slots // NBLOCK,)),
                ],
                compiler_params=pltpu.CompilerParams(vmem_limit_bytes=60 * 2**20),
                name="source_first",
            )(
                spectra,
                wind_growth.reshape(1, slots),
                wind_dir.reshape(1, slots),
                point_cell.reshape(1, slots),
            )
        else:
            message = pl.pallas_call(
                functools.partial(later_source_kernel, plan, first, count, nfreq),
                out_shape=shape,
                in_specs=[pl.BlockSpec((pl.Element(count), pl.Element(ndir), pl.Element(slots)), lambda i, s=first: (s, 0, 0))]
                + [pl.BlockSpec((ndir, slots), lambda i: (0, 0)), pl.BlockSpec((1, slots), lambda i: (0, 0))],
                out_specs=pl.BlockSpec(shape.shape, lambda i: (0, 0, 0)),
                grid=(1,),
                scratch_shapes=scratch,
                compiler_params=params(),
                name="source_later",
            )(spectra, gain, target)
        messages.append(message)

    whole = jax.ShapeDtypeStruct((nfreq, ndir, SUB, LANES), F32)
    grids = (shoaling, slope_x, slope_y, land_mask)
    lat = lax.axis_index("lat")
    lat_ids = jnp.stack(
        [
            jnp.maximum(lat - 1, 0),
            jnp.minimum(lat + 1, lat_count - 1),
            (lat > 0).astype(jnp.int32),
            (lat < lat_count - 1).astype(jnp.int32),
            lax.axis_index("lon") & 1,
        ]
    )
    label = None
    out = None

    def place(i, arrived):
        first, count, plan = starts[i], CHUNKS[i], plans[i]
        outs = [jax.ShapeDtypeStruct((count * ndir * SUB, LANES), F32)] + edge_shapes(count, ndir)
        if i == 0:
            outs.append(jax.ShapeDtypeStruct((1, slots), jnp.int32))
        field, *sent = pl.pallas_call(
            functools.partial(place_kernel, plan, first, count, ndir, i == 0),
            out_shape=outs,
            in_specs=vmem(1) + [SMEM_SPEC, SMEM_SPEC] + vmem(1 if i == 0 else 2),
            out_specs=vmem(len(outs)),
            scratch_shapes=[
                pltpu.VMEM((plan.total, slots), F32),
                pltpu.VMEM((2 * plan.total, slots), BF16),
            ],
            compiler_params=params(),
            name="place",
        )(arrived, speed, lat_ids, shoaling, *([] if i == 0 else [label]))
        return field.reshape(count, ndir, SUB, LANES), sent

    def step(i, field, received, side_first):
        same = jax.ShapeDtypeStruct(field.shape, F32)
        field, *sent = pl.pallas_call(
            functools.partial(step_kernel, starts[i], side_first, False),
            out_shape=[same] + edge_shapes(CHUNKS[i], ndir),
            in_specs=vmem(4) + [SMEM_SPEC, SMEM_SPEC] + vmem(4),
            out_specs=vmem(4),
            scratch_shapes=[pltpu.VMEM((ndir, SUB, LANES), F32)],
            compiler_params=params(),
            name="step",
        )(field, *received, speed, lat_ids, *grids)
        return field, sent

    def last_step(i, field, received, side_first, out, after=()):
        chained = out is not None
        return pl.pallas_call(
            functools.partial(step_kernel, starts[i], side_first, True),
            out_shape=whole,
            in_specs=vmem(4) + [SMEM_SPEC, SMEM_SPEC] + vmem(4) + [ANY_SPEC] * (len(after) + chained),
            out_specs=ANY_SPEC,
            scratch_shapes=[
                pltpu.VMEM(field.shape, F32),
                pltpu.VMEM((ndir, SUB, LANES), F32),
                pltpu.SemaphoreType.DMA((CHUNKS[i],)),
            ],
            input_output_aliases={10: 0} if chained else {},
            compiler_params=params(),
            name="last_step",
        )(field, *received, speed, lat_ids, *grids, *([out] if chained else []), *after)

    n = len(CHUNKS)
    tie = lax.optimization_barrier
    waiting = None
    for i in range(n):
        arrived = lax.all_to_all(
            messages[i], ("lon", "lat"), split_axis=0, concat_axis=0, tiled=True
        )
        if i + 1 < n:
            arrived, messages[i + 1] = tie((arrived, messages[i + 1]))
        if i >= 2:
            arrived, out = tie((arrived, out))
        field, sent = place(i, arrived)
        if i == 0:
            *sent, label = sent
        received = send_edges(*sent[:2])
        if waiting is None:
            sides = lax.all_gather(sent[2], "lat")
            side_first = 0
        else:
            sides = lax.all_gather(jnp.concatenate([waiting[2], sent[2]], axis=0), "lat")
            side_first = CHUNKS[i - 1]
            if i < n - 1:
                out = last_step(i - 1, waiting[0], (*waiting[1], sides), 0, out)
            else:
                pending = (i - 1, waiting[0], (*waiting[1], sides), 0, out)
        field, sent = step(i, field, (*received, sides), side_first)
        if i + 2 < n:
            *sent, messages[i + 2] = tie((*sent, messages[i + 2]))
        waiting = (field, send_edges(*sent[:2]), sent[2])
    field, received, side = waiting
    sides = lax.all_gather(side, "lat")
    out = last_step(*pending, (sides,))
    out = last_step(n - 1, field, (*received, sides), 0, out)
    bands = rows_y // LANES
    out = out.reshape(nfreq, ndir, bands, rows_x, LANES)
    return out.transpose(0, 1, 3, 2, 4).reshape(nfreq, ndir, rows_x, rows_y)


def solution(mesh):
    placed = (
        P(None, None, ("lon", "lat")),
        P(("lon", "lat")),
        P(("lon", "lat")),
        P(("lon", "lat")),
        P("lon", "lat"),
        P("lon", "lat"),
        P("lon", "lat"),
        P("lon", "lat"),
    )
    return jax.shard_map(
        on_device,
        mesh=mesh,
        in_specs=placed,
        out_specs=P(None, None, "lon", "lat"),
        check_vma=False,
    )
```

```python
import functools
import math

import jax
import jax.numpy as jnp
import numpy as np
from jax import lax
from jax.experimental import pallas as pl
from jax.experimental.pallas import tpu as pltpu
from jax.sharding import PartitionSpec as P

F32 = jnp.float32
BF16 = jnp.bfloat16
LANES = 128
SUB = 8
CHUNKS = (10, 8, 7)
NBLOCK = 256
VMEM_LIMIT = 32 * 2**20


def ceil_to(value, step):
    return -(-value // step) * step


def divide(value, count):
    if count & (count - 1) == 0:
        return value >> (count.bit_length() - 1), value & (count - 1)
    quotient = value // count
    return quotient, value - quotient * count


class Plan:
    def __init__(self, count, ndir, cap, labels):
        self.cap = cap
        self.parts = LANES // cap
        self.rows = count * ndir + (1 if labels else 0)
        self.per = -(-self.rows // self.parts)
        self.padded = ceil_to(self.per, SUB)
        self.total = self.parts * self.padded
        self.label_row = (
            count * ndir // self.per * self.padded + count * ndir % self.per if labels else None
        )

    def pieces(self, start, length):
        found = []
        at = start
        while at < start + length:
            part, inside = divmod(at, self.per)
            take = min(self.per - inside, start + length - at)
            found.append((at - start, part * self.padded + inside, take))
            at += take
        return found


def swap_blocks(blocks, cap):
    parts = len(blocks)
    lane = lax.broadcasted_iota(jnp.int32, blocks[0].shape, 1)
    rolled = [pltpu.roll(b, cap * q, 1) if q else b for q, b in enumerate(blocks)]
    result = []
    for i in range(parts):
        mixed = rolled[-i % parts]
        for j in range(1, parts):
            mixed = jnp.where(lane >= j * cap, rolled[(j - i) % parts], mixed)
        result.append(pltpu.roll(mixed, LANES - cap * i, 1) if i else mixed)
    return result


def split_rows(x_ref, pair_ref):
    total = x_ref.shape[0]
    whole = x_ref[...]
    high = whole.astype(BF16)
    pair_ref[0:total, :] = high
    pair_ref[total : 2 * total, :] = (whole - high.astype(F32)).astype(BF16)


def route(pair_ref, picks, first):
    slots = pair_ref.shape[1]
    total = pair_ref.shape[0] // 2
    wanted = lax.broadcasted_iota(jnp.int32, (NBLOCK, slots), 0) + first
    onehot = jnp.where(wanted == picks, 1.0, 0.0).astype(BF16)
    both = lax.dot_general(
        pair_ref[...], onehot, (((1,), (1,)), ((), ())), preferred_element_type=F32
    )
    return both[:total] + both[total:]


def send_rows(plan, pair_ref, target, out_ref, done=None):
    slots = pair_ref.shape[1]
    groups = NBLOCK // LANES
    for block in range(slots // NBLOCK):
        moved = route(pair_ref, target, block * NBLOCK)
        for g in range(groups):
            blocks = [
                moved[q * plan.padded : (q + 1) * plan.padded, g * LANES : (g + 1) * LANES]
                for q in range(plan.parts)
            ]
            for i, message in enumerate(swap_blocks(blocks, plan.cap)):
                out_ref[(block * groups + g) * plan.parts + i] = message
        if done is not None:
            done(block)


def source_rows(plan, spectra_ref, first, count, nfreq, gain, x_ref):
    ndir = spectra_ref.shape[1]
    for f in range(count):
        ratio = float(np.float32(1.1) ** np.float32(first + f - (nfreq - 1)))
        rows = spectra_ref[f] * jnp.exp(gain * ratio)
        for offset, row, length in plan.pieces(f * ndir, ndir):
            x_ref[row : row + length, :] = rows[offset : offset + length]


PIECES = 5


def first_source_kernel(
    plan, count, shape, spectra_hbm, growth_hbm, dir_hbm, cell_hbm,
    out_hbm, gain_ref, target_ref,
    spectra_ref, growth_ref, dir_ref, cell_ref, x_ref, pair_ref, message_ref, sems, out_sems,
):
    rows_x, rows_y, lat_count, devices = shape
    nfreq, ndir, slots = spectra_ref.shape
    bounds = [nfreq * k // PIECES for k in range(PIECES + 1)]
    small = [
        pltpu.make_async_copy(src, dst, sems.at[PIECES + k])
        for k, (src, dst) in enumerate(
            ((cell_hbm, cell_ref), (growth_hbm, growth_ref), (dir_hbm, dir_ref))
        )
    ]
    pieces = [
        pltpu.make_async_copy(
            spectra_hbm.at[pl.ds(lo, hi - lo)], spectra_ref.at[pl.ds(lo, hi - lo)], sems.at[k]
        )
        for k, (lo, hi) in enumerate(zip(bounds, bounds[1:]))
    ]
    for copy in small + pieces:
        copy.start()
    small[0].wait()
    point = cell_ref[...]
    valid = point >= 0
    col_x, col_y = divide(jnp.maximum(point, 0), rows_y * lat_count)
    own_x, in_x = divide(col_x, rows_x)
    own_y, in_y = divide(col_y, rows_y)
    owner = jnp.where(valid, own_x * lat_count + own_y, devices)
    band, lane = divide(in_y, LANES)
    label = jnp.where(valid, (band * rows_x + in_x) * LANES + lane + 1, 0).astype(F32)
    ids = lax.broadcasted_iota(jnp.int32, (devices, slots), 0)
    hits = jnp.where(ids == owner, 1.0, 0.0)
    lower = lax.broadcasted_iota(jnp.int32, (LANES, LANES), 0) < lax.broadcasted_iota(
        jnp.int32, (LANES, LANES), 1
    )
    ahead = jnp.where(lower, 1.0, 0.0).astype(BF16)
    carry = jnp.zeros((devices, 1), F32)
    places = []
    for b in range(slots // LANES):
        part = hits[:, b * LANES : (b + 1) * LANES]
        before = jnp.dot(part.astype(BF16), ahead, preferred_element_type=F32) + carry
        places.append(jnp.sum(before * part, axis=0, keepdims=True))
        carry = carry + jnp.sum(part, axis=1, keepdims=True)
    place = jnp.concatenate(places, axis=1).astype(jnp.int32)
    target = jnp.where(valid, owner * plan.cap + place, slots)
    target_ref[...] = target

    small[1].wait()
    small[2].wait()
    dtheta = 2.0 * math.pi / ndir
    total = None
    for k, copy in enumerate(pieces):
        copy.wait()
        for f in range(bounds[k], bounds[k + 1]):
            width = float(np.float32(0.1) * np.float32(1.1) ** np.float32(f)) * dtheta
            term = spectra_ref[f] * width
            total = term if total is None else total + term
    energy = jnp.sum(total, axis=0, keepdims=True)
    load = energy / (energy + 10.0)
    theta = (lax.broadcasted_iota(jnp.int32, (ndir, slots), 0).astype(F32) + 0.5) * dtheta
    lobe = jnp.maximum(jnp.cos(theta - dir_ref[...]), 0.0)
    gain = growth_ref[...] * (lobe * lobe) - 0.4 * load
    gain_ref[...] = gain

    source_rows(plan, spectra_ref, 0, count, nfreq, gain, x_ref)
    x_ref[plan.label_row : plan.label_row + 1, :] = label
    split_rows(x_ref, pair_ref)
    copies = []

    def sent(block):
        per = devices * NBLOCK // slots
        part = pl.ds(block * per, per)
        copies.append(
            pltpu.make_async_copy(message_ref.at[part], out_hbm.at[part], out_sems.at[block])
        )
        copies[-1].start()

    send_rows(plan, pair_ref, target, message_ref, sent)
    for copy in copies:
        copy.wait()


def later_source_kernel(
    plan, first, count, nfreq, spectra_ref, gain_ref, target_ref, out_ref, x_ref, pair_ref
):
    source_rows(plan, spectra_ref, first, count, nfreq, gain_ref[...], x_ref)
    split_rows(x_ref, pair_ref)
    send_rows(plan, pair_ref, target_ref[...], out_ref)


def as_tile(grid_ref):
    grid = grid_ref[...].astype(F32)
    bands = grid.shape[1] // LANES
    return jnp.concatenate([grid[:, b * LANES : (b + 1) * LANES] for b in range(bands)], axis=0)


def tile_ids():
    return (
        lax.broadcasted_iota(jnp.int32, (SUB, LANES), 0),
        lax.broadcasted_iota(jnp.int32, (SUB, LANES), 1),
    )


def edge_messages(read, weight, odd_lon, f, ndir, near_ref, cross_ref, side_ref):
    row, lane = tile_ids()
    odd = (row & 1) == 1
    quarter = ndir // 4
    up = jnp.zeros((SUB, LANES), F32)
    down = jnp.zeros((SUB, LANES), F32)
    moved = [read(d) * weight for d in range(ndir)]
    for e in range(quarter):
        a, b = moved[3 * quarter + e], moved[e]
        right = jnp.where(odd, b, pltpu.roll(a, SUB - 1, 0))
        a, b = moved[quarter + e], moved[2 * quarter + e]
        left = jnp.where(odd, pltpu.roll(b, 1, 0), a)
        near_ref[f, e] = jnp.where(odd_lon, left, right)
        cross_ref[f, e] = jnp.where(odd_lon, right, left)
    for k in range(2 * quarter):
        up = jnp.where(lane == k, pltpu.roll(moved[k], k + 1, 1), up)
        low = moved[2 * quarter + k]
        down = jnp.where(lane == k, pltpu.roll(low, k, 1) if k else low, down)
    side_ref[f] = jnp.where(row >= SUB // 2, up, down)


def place_kernel(plan, first, count, ndir, with_labels, *refs):
    if with_labels:
        in_ref, speed_ref, ids_ref, shoal_ref, *refs = refs
        own_ref, near_ref, cross_ref, side_ref, label_ref, x_ref, pair_ref = refs
    else:
        in_ref, speed_ref, ids_ref, shoal_ref, label_ref, *refs = refs
        own_ref, near_ref, cross_ref, side_ref, x_ref, pair_ref = refs
    slots = x_ref.shape[1]
    for g in range(slots // LANES):
        blocks = [in_ref[g * plan.parts + i] for i in range(plan.parts)]
        for q, part in enumerate(swap_blocks(blocks, plan.cap)):
            x_ref[q * plan.padded : (q + 1) * plan.padded, g * LANES : (g + 1) * LANES] = part
    if with_labels:
        label_ref[...] = x_ref[plan.label_row : plan.label_row + 1, :].astype(jnp.int32) - 1
    label = label_ref[...]
    split_rows(x_ref, pair_ref)
    for block in range(slots // NBLOCK):
        placed = route(pair_ref, label, block * NBLOCK)
        for t in range(NBLOCK // LANES):
            row = block * (NBLOCK // LANES) + t
            for q in range(plan.parts):
                length = min(plan.per, count * ndir - q * plan.per)
                if length > 0:
                    own_ref[pl.ds(q * plan.per * SUB + row, length, stride=SUB), :] = placed[
                        q * plan.padded : q * plan.padded + length, t * LANES : (t + 1) * LANES
                    ]
    shoal = as_tile(shoal_ref)

    @pl.loop(0, count)
    def pack(f):
        def read(d):
            return own_ref[pl.ds(pl.multiple_of((f * ndir + d) * SUB, SUB), SUB), :]

        edge_messages(
            read, shoal * speed_ref[first + f], ids_ref[4] == 1, f, ndir, near_ref, cross_ref, side_ref
        )


def step_kernel(first, side_first, last, *refs):
    (own_ref, pair_in, cross_in, side_in, speed_ref, lat_ref,
     shoal_ref, slope_x_ref, slope_y_ref, mask_ref, *refs) = refs
    if last:
        out_ref, new_ref, turn_ref, done_sem = refs[-4:]
    else:
        new_ref, near_ref, cross_ref, side_ref, turn_ref = refs
    count, ndir = own_ref.shape[:2]
    quarter = ndir // 4
    row, lane = tile_ids()
    odd = (row & 1) == 1
    shoal = as_tile(shoal_ref)
    slope_x = as_tile(slope_x_ref)
    slope_y = as_tile(slope_y_ref)
    sea = as_tile(mask_ref)
    angle = [(d + 0.5) * (2.0 * math.pi / ndir) for d in range(ndir)]
    cos = [math.cos(a) for a in angle]
    sin = [math.sin(a) for a in angle]
    for d in range(ndir):
        turn_ref[d] = sin[d] * slope_x - cos[d] * slope_y

    odd_lon = lat_ref[4] == 1
    keep_up = lat_ref[2].astype(F32)
    keep_down = lat_ref[3].astype(F32)

    def write(f):
        return pltpu.make_async_copy(new_ref.at[f], out_ref.at[first + f], done_sem.at[f])

    @pl.loop(0, count)
    def advance(f):
        speed = speed_ref[first + f]
        weight = shoal * speed
        up_all = side_in[lat_ref[0], side_first + f] * keep_up
        down_all = side_in[lat_ref[1], side_first + f] * keep_down

        def halved(d):
            field = own_ref[f, d]
            moved = weight * field
            if d >= 3 * quarter or d < quarter:
                edge = jnp.where(odd_lon, pair_in[f, d % quarter], cross_in[f, d % quarter])
                if d < quarter:
                    edge = pltpu.roll(edge, SUB - 1, 0)
                from_x = jnp.where(odd, pltpu.roll(moved, 1, 0), edge)
            else:
                edge = jnp.where(odd_lon, cross_in[f, d % quarter], pair_in[f, d % quarter])
                if d < 2 * quarter:
                    edge = pltpu.roll(edge, 1, 0)
                from_x = jnp.where(odd, edge, pltpu.roll(moved, SUB - 1, 0))
            if d < 2 * quarter:
                near = pltpu.roll(moved, 1, 1)
                edge = pltpu.roll(up_all, LANES - d, 1) if d else up_all
                far = pltpu.roll(jnp.where(row >= SUB - 2, edge, near), 2, 0)
                from_y = jnp.where(lane == 0, far, near)
            else:
                near = pltpu.roll(moved, LANES - 1, 1)
                edge = pltpu.roll(down_all, LANES - 1 - (d - 2 * quarter), 1)
                far = pltpu.roll(jnp.where(row < 2, edge, near), SUB - 2, 0)
                from_y = jnp.where(lane == LANES - 1, far, near)
            along, across = abs(cos[d]), abs(sin[d])
            half = field - (along + across) * moved + along * from_x + across * from_y
            return half, turn_ref[d] * (half * speed)

        half_top, qt_top = halved(ndir - 1)
        half, qt = halved(0)
        below = jnp.maximum(qt_top, 0.0) + jnp.minimum(qt, 0.0)
        flux_top = below
        for d in range(ndir):
            if d < ndir - 2:
                half_next, qt_next = halved(d + 1)
            else:
                half_next, qt_next = half_top, qt_top
            if d < ndir - 1:
                above = jnp.maximum(qt, 0.0) + jnp.minimum(qt_next, 0.0)
            else:
                above = flux_top
            new_ref[f, d] = (half - above + below) * sea
            half, qt, below = half_next, qt_next, above
        if not last:
            edge_messages(
                lambda d: new_ref[f, d], weight, odd_lon, f, ndir, near_ref, cross_ref, side_ref
            )
        if last:
            write(f).start()

    if last:

        @pl.loop(0, count)
        def finish(f):
            write(f).wait()


def params():
    return pltpu.CompilerParams(vmem_limit_bytes=VMEM_LIMIT)


def vmem(count):
    return [pl.BlockSpec(memory_space=pltpu.VMEM)] * count


SMEM_SPEC = pl.BlockSpec(memory_space=pltpu.SMEM)
ANY_SPEC = pl.BlockSpec(memory_space=pl.ANY)
HBM_SPEC = pl.BlockSpec(memory_space=pltpu.HBM)


def edge_shapes(count, ndir):
    tile = jax.ShapeDtypeStruct((count, ndir // 4, SUB, LANES), F32)
    line = jax.ShapeDtypeStruct((count, SUB, LANES), F32)
    return [tile, tile, line]


def send_edges(pair, cross):
    lon = lax.axis_size("lon")
    return (
        lax.ppermute(pair, "lon", [(i, i ^ 1) for i in range(lon)]),
        lax.ppermute(cross, "lon", [(i, (i + 2 * (i & 1) - 1) % lon) for i in range(lon)]),
    )


def on_device(spectra, wind_growth, wind_dir, point_cell, land_mask, shoaling, slope_x, slope_y):
    nfreq, ndir, slots = spectra.shape
    rows_x, rows_y = land_mask.shape
    lat_count = lax.axis_size("lat")
    devices = lax.axis_size("lon") * lat_count
    cap = slots // devices
    speed = jnp.asarray((0.65 * 1.1 ** -np.arange(nfreq)).astype(np.float32))
    starts = [sum(CHUNKS[:i]) for i in range(len(CHUNKS))]
    plans = [Plan(count, ndir, cap, i == 0) for i, count in enumerate(CHUNKS)]

    messages = []
    for i, (first, count, plan) in enumerate(zip(starts, CHUNKS, plans)):
        shape = jax.ShapeDtypeStruct((devices, plan.padded, LANES), F32)
        scratch = [
            pltpu.VMEM((plan.total, slots), F32),
            pltpu.VMEM((2 * plan.total, slots), BF16),
        ]
        if i == 0:
            message, gain, target = pl.pallas_call(
                functools.partial(
                    first_source_kernel, plan, count, (rows_x, rows_y, lat_count, devices)
                ),
                out_shape=[
                    shape,
                    jax.ShapeDtypeStruct((ndir, slots), F32),
                    jax.ShapeDtypeStruct((1, slots), jnp.int32),
                ],
                in_specs=[HBM_SPEC] * 4,
                out_specs=[HBM_SPEC] + vmem(2),
                scratch_shapes=[
                    pltpu.VMEM(spectra.shape, F32),
                    pltpu.VMEM((1, slots), F32),
                    pltpu.VMEM((1, slots), F32),
                    pltpu.VMEM((1, slots), jnp.int32),
                    *scratch,
                    pltpu.VMEM(shape.shape, F32),
                    pltpu.SemaphoreType.DMA((PIECES + 3,)),
                    pltpu.SemaphoreType.DMA((slots // NBLOCK,)),
                ],
                compiler_params=pltpu.CompilerParams(vmem_limit_bytes=60 * 2**20),
                name="source_first",
            )(
                spectra,
                wind_growth.reshape(1, slots),
                wind_dir.reshape(1, slots),
                point_cell.reshape(1, slots),
            )
        else:
            message = pl.pallas_call(
                functools.partial(later_source_kernel, plan, first, count, nfreq),
                out_shape=shape,
                in_specs=[pl.BlockSpec((pl.Element(count), pl.Element(ndir), pl.Element(slots)), lambda i, s=first: (s, 0, 0))]
                + [pl.BlockSpec((ndir, slots), lambda i: (0, 0)), pl.BlockSpec((1, slots), lambda i: (0, 0))],
                out_specs=pl.BlockSpec(shape.shape, lambda i: (0, 0, 0)),
                grid=(1,),
                scratch_shapes=scratch,
                compiler_params=pltpu.CompilerParams(vmem_limit_bytes=60 * 2**20),
                name="source_later",
            )(spectra, gain, target)
        messages.append(message)

    whole = jax.ShapeDtypeStruct((nfreq, ndir, SUB, LANES), F32)
    grids = (shoaling, slope_x, slope_y, land_mask)
    lat = lax.axis_index("lat")
    lat_ids = jnp.stack(
        [
            jnp.maximum(lat - 1, 0),
            jnp.minimum(lat + 1, lat_count - 1),
            (lat > 0).astype(jnp.int32),
            (lat < lat_count - 1).astype(jnp.int32),
            lax.axis_index("lon") & 1,
        ]
    )
    label = None
    out = None

    def place(i, arrived):
        first, count, plan = starts[i], CHUNKS[i], plans[i]
        outs = [jax.ShapeDtypeStruct((count * ndir * SUB, LANES), F32)] + edge_shapes(count, ndir)
        if i == 0:
            outs.append(jax.ShapeDtypeStruct((1, slots), jnp.int32))
        field, *sent = pl.pallas_call(
            functools.partial(place_kernel, plan, first, count, ndir, i == 0),
            out_shape=outs,
            in_specs=vmem(1) + [SMEM_SPEC, SMEM_SPEC] + vmem(1 if i == 0 else 2),
            out_specs=vmem(len(outs)),
            scratch_shapes=[
                pltpu.VMEM((plan.total, slots), F32),
                pltpu.VMEM((2 * plan.total, slots), BF16),
            ],
            compiler_params=params(),
            name="place",
        )(arrived, speed, lat_ids, shoaling, *([] if i == 0 else [label]))
        return field.reshape(count, ndir, SUB, LANES), sent

    def step(i, field, received, side_first):
        same = jax.ShapeDtypeStruct(field.shape, F32)
        field, *sent = pl.pallas_call(
            functools.partial(step_kernel, starts[i], side_first, False),
            out_shape=[same] + edge_shapes(CHUNKS[i], ndir),
            in_specs=vmem(4) + [SMEM_SPEC, SMEM_SPEC] + vmem(4),
            out_specs=vmem(4),
            scratch_shapes=[pltpu.VMEM((ndir, SUB, LANES), F32)],
            compiler_params=params(),
            name="step",
        )(field, *received, speed, lat_ids, *grids)
        return field, sent

    def last_step(i, field, received, side_first, out, after=()):
        chained = out is not None
        return pl.pallas_call(
            functools.partial(step_kernel, starts[i], side_first, True),
            out_shape=whole,
            in_specs=vmem(4) + [SMEM_SPEC, SMEM_SPEC] + vmem(4) + [ANY_SPEC] * (len(after) + chained),
            out_specs=ANY_SPEC,
            scratch_shapes=[
                pltpu.VMEM(field.shape, F32),
                pltpu.VMEM((ndir, SUB, LANES), F32),
                pltpu.SemaphoreType.DMA((CHUNKS[i],)),
            ],
            input_output_aliases={10: 0} if chained else {},
            compiler_params=params(),
            name="last_step",
        )(field, *received, speed, lat_ids, *grids, *([out] if chained else []), *after)

    n = len(CHUNKS)
    tie = lax.optimization_barrier
    waiting = None
    for i in range(n):
        arrived = lax.all_to_all(
            messages[i], ("lon", "lat"), split_axis=0, concat_axis=0, tiled=True
        )
        if i + 1 < n:
            arrived, messages[i + 1] = tie((arrived, messages[i + 1]))
        if i >= 2:
            arrived, out = tie((arrived, out))
        field, sent = place(i, arrived)
        if i == 0:
            *sent, label = sent
        received = send_edges(*sent[:2])
        if waiting is None:
            sides = lax.all_gather(sent[2], "lat")
            side_first = 0
        else:
            sides = lax.all_gather(jnp.concatenate([waiting[2], sent[2]], axis=0), "lat")
            side_first = CHUNKS[i - 1]
            if i < n - 1:
                out = last_step(i - 1, waiting[0], (*waiting[1], sides), 0, out)
            else:
                pending = (i - 1, waiting[0], (*waiting[1], sides), 0, out)
        field, sent = step(i, field, (*received, sides), side_first)
        if i + 2 < n:
            *sent, messages[i + 2] = tie((*sent, messages[i + 2]))
        waiting = (field, send_edges(*sent[:2]), sent[2])
    field, received, side = waiting
    sides = lax.all_gather(side, "lat")
    out = last_step(*pending, (sides,))
    out = last_step(n - 1, field, (*received, sides), 0, out)
    bands = rows_y // LANES
    out = out.reshape(nfreq, ndir, bands, rows_x, LANES)
    return out.transpose(0, 1, 3, 2, 4).reshape(nfreq, ndir, rows_x, rows_y)


def solution(mesh):
    placed = (
        P(None, None, ("lon", "lat")),
        P(("lon", "lat")),
        P(("lon", "lat")),
        P(("lon", "lat")),
        P("lon", "lat"),
        P("lon", "lat"),
        P("lon", "lat"),
        P("lon", "lat"),
    )
    return jax.shard_map(
        on_device,
        mesh=mesh,
        in_specs=placed,
        out_specs=P(None, None, "lon", "lat"),
        check_vma=False,
    )
```
